32 devices in a mesh: dp: 2 (over y), expert: 16 (over z, x, core).
Axes of the slice: x: 2, y: 2, z: 4, core: 2. Of those that a mesh axis runs over, the one named last changes fastest.
Arguments:
- tokens: bfloat16 [1024, 2048], P(('dp', 'expert')), may hold values from -6 to 6
- routes: int32 [1024, 8], P(('dp', 'expert')), may hold values from 0 to 15, all different within a row; in each aligned block of 32 rows (0 to 31, 32 to 63, ...) at most 32 rows name the same one
- cotangent: bfloat16 [1024, 2048], P(('dp', 'expert')), may hold values from -6 to 6
- router_weight: bfloat16 [2048, 16], replicated, may hold values from -0.375 to 0.375
- gate_weight: bfloat16 [16, 2048, 768], P('expert'), may hold values from -0.125 to 0.125
- up_weight: bfloat16 [16, 2048, 768], P('expert'), may hold values from -0.125 to 0.125
- down_weight: bfloat16 [16, 768, 2048], P('expert'), may hold values from -0.21875 to 0.21875
Outputs:
- layer_out: bfloat16 [1024, 2048], P(('dp', 'expert'))
- token_grad: bfloat16 [1024, 2048], P(('dp', 'expert'))
- gate_grad: bfloat16 [16, 2048, 768], P('expert', 'dp')
- up_grad: bfloat16 [16, 2048, 768], P('expert', 'dp')
- down_grad: bfloat16 [16, 768, 2048], P('expert', None, 'dp')
- router_grad: float32 [2048, 16], replicated
The draws below stay inside these ranges and needn't reach their ends.
Inputs may be any that keep to these rules, and one draw needn't show every extreme that they name: `routes`: each row names 8 different experts. Among the 32 rows of one device no expert is named by more than 32 rows, and in some device's rows an expert is named by exactly 32 rows.
All inputs are finite; a program needn't handle non-finite values.
Results may differ from the reference program's by a relative error of at most 0.0061.
Values may be sent and summed in bfloat16 or wider, within the bound.
A program may use at most 128 MiB of HBM per device.

```python
import math
import jax
import jax.numpy as jnp
import numpy as np
from jax import lax

D = 2048
F = 768
TOPK = 8
TOK_DEV = 32
EXPERTS = 16
CAP = 32
TOKENS = 1024


def levels(rng, extent, cuts, least, high):
    gain = 1.0
    for axis_at, blocks in cuts:
        heights = jax.random.uniform(jax.random.fold_in(jax.random.fold_in(rng, 6), axis_at), (blocks,), jnp.float32, least / len(cuts), high / len(cuts))
        gain = gain * jnp.repeat(jnp.exp(heights), extent[axis_at] // blocks).reshape((-1,) + (1,) * (len(extent) - 1 - axis_at))
    return gain


def deal_out(stream_key, own, number, rows, amount, top, bound, lean):
    sequence = jax.random.permutation(stream_key, amount)
    crowded, ordinary = portions_of(amount, rows * top, bound, lean, True), portions_of(amount, rows * top, bound, lean, False)
    places = jnp.arange(amount)

    def named(sizes, rotation):
        used = int((sizes > 0).sum())
        fixed = max(1, used // 4)
        shifted = fixed + (places - fixed + rotation * (used - fixed)) % max(1, amount - fixed)
        return jnp.zeros((amount,), jnp.int32).at[sequence[jnp.where(places < fixed, places, shifted)]].set(jnp.asarray(sizes, jnp.int32))

    sizes = jnp.where(number % 4 == 0, named(crowded, number // 4), named(ordinary, number - number // 4 - 1))
    mixed = jax.random.permutation(jax.random.fold_in(own, 3), amount)
    donor, sink = mixed[0:amount // 2 * 2:2], mixed[1:amount // 2 * 2:2]
    slack = jnp.minimum(sizes[donor] - 1, bound - sizes[sink]) // 2
    slack = jnp.where((donor == sequence[0]) | (sink == sequence[0]) | (sizes[sink] == 0), 0, jnp.maximum(slack, 0))
    shifted = jax.random.randint(jax.random.fold_in(own, 4), (amount // 2,), 0, 1 << 20) % (slack + 1)
    sizes = sizes.at[donor].add(-shifted).at[sink].add(shifted)
    members = jnp.searchsorted(jnp.cumsum(sizes), jnp.arange(rows * top), side="right").astype(jnp.int32)
    grid = members.reshape(top, rows).T
    grid = grid[jax.random.permutation(jax.random.fold_in(own, 1), rows)]
    rotation = jax.random.randint(jax.random.fold_in(own, 2), (rows, 1), 0, top)
    return jnp.take_along_axis(grid, (jnp.arange(top)[None, :] + rotation) % top, axis=1)


def portions_of(number_of, total, limit, skew, full):
    loads = [(1 << 20) // math.isqrt(grade ** skew) + 1 for grade in range(1, number_of + 1)]
    largest = limit if full else min(limit, max(-(-total // number_of), total * loads[0] // sum(loads)))
    least = 1 if total - largest >= number_of - 1 else 0
    given, surplus = [largest] + [least] * (number_of - 1), total - largest - least * (number_of - 1)
    while surplus > 0:
        free = [i for i in range(1, number_of) if given[i] < largest] or [i for i in range(1, number_of) if given[i] < limit]
        pool, budget = sum([loads[i] for i in free]), surplus
        for i in free:
            more = min(limit - given[i], max(1, budget * loads[i] // pool), surplus)
            given[i] = given[i] + more
            surplus = surplus - more
    return np.array(given)


def scatter_about(own_key, shape, scale, limit, split=(), kind=jnp.bfloat16):
    drawn = scale * jax.random.normal(own_key, shape, jnp.float32)
    if split:
        drawn = drawn * levels(own_key, shape, split, -0.22, 0.18)
    return jnp.clip(drawn, -limit, limit).astype(kind)


def setup_inputs(seed: int = 0) -> dict:
    arg_keys = jax.random.split(jax.random.key(seed), 8)
    tokens = scatter_about(arg_keys[0], (TOKENS, D), 1.0, 6.0, ((0, 32),))
    routes_keys = jax.random.split(jax.random.fold_in(arg_keys[1], 1), TOKENS // TOK_DEV)
    routes_turns = jax.random.permutation(jax.random.fold_in(arg_keys[1], 3), TOKENS // TOK_DEV)
    routes = jax.vmap(lambda own, number: deal_out(jax.random.fold_in(arg_keys[1], 2), own, number, TOK_DEV, EXPERTS, TOPK, CAP, 2))(routes_keys, routes_turns).reshape((TOKENS, TOPK))
    cotangent = scatter_about(arg_keys[2], (TOKENS, D), 1.0, 6.0, ((0, 32),))
    router_weight = scatter_about(arg_keys[3], (D, EXPERTS), (D // 9) ** -0.5, 0.375)
    gate_weight = scatter_about(arg_keys[4], (EXPERTS, D, F), D ** -0.5, 0.125, ((0, 16),))
    up_weight = scatter_about(arg_keys[5], (EXPERTS, D, F), D ** -0.5, 0.125, ((0, 16),))
    down_weight = scatter_about(arg_keys[6], (EXPERTS, F, D), F ** -0.5, 0.21875, ((0, 16),))
    return {"tokens": tokens, "routes": routes, "cotangent": cotangent, "router_weight": router_weight, "gate_weight": gate_weight, "up_weight": up_weight, "down_weight": down_weight}


def silu_parts(gate_act):
    sigmoid_value = jax.nn.sigmoid(gate_act)
    act_value = gate_act * sigmoid_value
    act_slope = sigmoid_value * (1.0 + gate_act * (1.0 - sigmoid_value))
    return act_value, act_slope


def reference(tokens, routes, cotangent, router_weight, gate_weight, up_weight, down_weight):
    tok_all, top_count = routes.shape
    expert_count = router_weight.shape[1]
    blocks = tok_all // TOK_DEV
    pair_count = tok_all * top_count
    logits = jnp.dot(tokens, router_weight, preferred_element_type=jnp.float32)
    exp_logits = jnp.exp(logits)
    probability = exp_logits / jnp.sum(exp_logits, axis=1, keepdims=True)
    chosen = (routes[:, :, None] == jnp.arange(expert_count, dtype=jnp.int32)[None, None, :]).astype(jnp.int32)
    chosen_blocks = chosen.reshape(blocks, TOK_DEV, top_count, expert_count)
    per_token = jnp.sum(chosen_blocks, axis=2).astype(jnp.int32)
    earlier = (jnp.cumsum(per_token, axis=1) - per_token).astype(jnp.int32)
    slot_ids = jnp.sum(chosen_blocks * earlier[:, :, None, :], axis=3).astype(jnp.int32).reshape(tok_all, top_count)
    block_of = (jnp.arange(tok_all, dtype=jnp.int32) // TOK_DEV).astype(jnp.int32)
    position = ((routes * blocks + block_of[:, None]) * CAP + slot_ids).astype(jnp.int32)
    slot_table = jnp.full((expert_count * blocks * CAP,), pair_count, dtype=jnp.int32)
    slot_table = slot_table.at[position.reshape(-1)].set(jnp.arange(pair_count, dtype=jnp.int32))
    slot_table = slot_table.reshape(expert_count, blocks * CAP)
    chosen_float = chosen.astype(jnp.float32)
    selected = jnp.sum(chosen_float * probability[:, None, :], axis=2)
    sel_total = jnp.sum(selected, axis=1, keepdims=True)
    combine = selected / sel_total
    zero_row = jnp.zeros((1, D), tokens.dtype)
    tokens_pad = jnp.concatenate([tokens, zero_row], axis=0)
    cot_pad = jnp.concatenate([cotangent, zero_row], axis=0)
    combine_pad = jnp.concatenate([combine.reshape(-1), jnp.zeros((1,), jnp.float32)])

    def expert_step(running, inputs):
        mixed_acc, grad_acc, comb_acc = running
        row_ids, gate_mat, up_mat, down_mat = inputs
        token_ids = (row_ids // top_count).astype(jnp.int32)
        slot_inputs = tokens_pad[token_ids]
        slot_cot = cot_pad[token_ids]
        slot_comb = combine_pad[row_ids]
        slot_grads = (slot_comb[:, None] * slot_cot.astype(jnp.float32)).astype(jnp.bfloat16)
        gate_act = jnp.dot(slot_inputs, gate_mat, preferred_element_type=jnp.float32)
        up_act = jnp.dot(slot_inputs, up_mat, preferred_element_type=jnp.float32)
        act_value, act_slope = silu_parts(gate_act)
        hidden = (act_value * up_act).astype(jnp.bfloat16)
        expert_out = jnp.dot(hidden, down_mat, preferred_element_type=jnp.float32).astype(jnp.bfloat16)
        hidden_grad = jnp.dot(slot_grads, down_mat.T, preferred_element_type=jnp.float32)
        gate_part = (hidden_grad * up_act * act_slope).astype(jnp.bfloat16)
        up_part = (hidden_grad * act_value).astype(jnp.bfloat16)
        input_grad = (jnp.dot(gate_part, gate_mat.T, preferred_element_type=jnp.float32)
                      + jnp.dot(up_part, up_mat.T, preferred_element_type=jnp.float32)).astype(jnp.bfloat16)
        gate_part_sum = jnp.dot(slot_inputs.T, gate_part, preferred_element_type=jnp.float32).astype(jnp.bfloat16)
        up_part_sum = jnp.dot(slot_inputs.T, up_part, preferred_element_type=jnp.float32).astype(jnp.bfloat16)
        down_part_sum = jnp.dot(hidden.T, slot_grads, preferred_element_type=jnp.float32).astype(jnp.bfloat16)
        out_float = expert_out.astype(jnp.float32)
        mixed_acc = mixed_acc.at[token_ids].add(slot_comb[:, None] * out_float)
        grad_acc = grad_acc.at[token_ids].add(input_grad.astype(jnp.float32))
        comb_acc = comb_acc.at[row_ids].add(jnp.sum(slot_cot.astype(jnp.float32) * out_float, axis=1))
        return (mixed_acc, grad_acc, comb_acc), (gate_part_sum, up_part_sum, down_part_sum)

    start_state = (jnp.zeros((tok_all + 1, D), jnp.float32),
                   jnp.zeros((tok_all + 1, D), jnp.float32),
                   jnp.zeros((pair_count + 1,), jnp.float32))
    final_state, weight_grads = lax.scan(expert_step, start_state, (slot_table, gate_weight, up_weight, down_weight))
    mixed_acc, grad_acc, comb_acc = final_state
    gate_grad, up_grad, down_grad = weight_grads
    layer_out = mixed_acc[:tok_all].astype(jnp.bfloat16)
    comb_grad = comb_acc[:pair_count].reshape(tok_all, top_count)
    sel_grad = (comb_grad - jnp.sum(combine * comb_grad, axis=1, keepdims=True)) / sel_total
    prob_grad = jnp.sum(chosen_float * sel_grad[:, :, None], axis=1)
    logit_grad = probability * (prob_grad - jnp.sum(probability * prob_grad, axis=1, keepdims=True))
    router_grad = jnp.dot(tokens.astype(jnp.float32).T, logit_grad, precision=lax.Precision.HIGHEST)
    router_back = jnp.dot(logit_grad, router_weight.astype(jnp.float32).T, precision=lax.Precision.HIGHEST)
    token_grad = (grad_acc[:tok_all] + router_back).astype(jnp.bfloat16)
    return (layer_out, token_grad, gate_grad, up_grad, down_grad, router_grad)
```

```python
import functools

import jax
import jax.numpy as jnp
from jax import lax
from jax.experimental import pallas as pl
from jax.experimental.pallas import tpu as pltpu
from jax.sharding import PartitionSpec as P

MESH = pl.DeviceIdType.MESH
NN = (((1,), (0,)), ((), ()))
NT = (((1,), (1,)), ((), ()))
TN = (((0,), (0,)), ((), ()))
F32 = jnp.float32
BF16 = jnp.bfloat16
TILE = 256
LANES = 128


def dot(a, b, dims):
    return lax.dot_general(a, b, dims, preferred_element_type=F32)


def split3(value):
    high = value.astype(BF16).astype(F32)
    middle = (value - high).astype(BF16).astype(F32)
    low = (value - high - middle).astype(BF16).astype(F32)
    return high, middle, low


class Book:
    def __init__(self):
        self.places = {}

    def __call__(self, *key):
        return self.places.setdefault(key, len(self.places))


COPIES = 110


def fused(
    experts, tok_ref, routes_ref, cot_ref, router_ref, gate_hbm, up_hbm, down_hbm,
    out_ref, tgrad_ref, gg_ref, ug_ref, dg_ref, rgrad_ref,
    tok_all, cot_all, gate_w, up_w, down_w, gate_t, up_t, down_t,
    hid, gpart, upart, out_p, in_p, core_o, core_i, x_o, x_i, z_o, z_i,
    lgs, acc_g, acc_u, acc_d, small, load_sem, send_sem, recv_sem, lg_send, lg_recv,
):
    rows, width = tok_ref.shape
    inner = gate_w.shape[1]
    half = gg_ref.shape[0]
    group = 4 * rows
    dp = lax.axis_index("dp")
    me = lax.axis_index("expert")
    z, x, core = me // 4, (me // 2) % 2, me % 2
    z_of = {0: z, 1: z + 1 - 2 * (z % 2), 2: (z + 2) % 4, 3: 3 - z}
    middle_chip = (z + 1) % 4 >= 2

    def device(ry=0, rz=0, rc=0, rx=0):
        return (
            1 - dp if ry else dp,
            z_of[rz] * 4 + (1 - x if rx else x) * 2 + (1 - core if rc else core),
        )

    barrier = pltpu.get_barrier_semaphore()
    others = [
        (ry, rz, rc, rx) for ry in range(2) for rz in range(4) for rc in range(2) for rx in range(2)
    ][1:]
    for rel in others:
        pl.semaphore_signal(barrier, inc=1, device_id=device(*rel), device_id_type=MESH)

    loads = [
        pltpu.make_async_copy(src, dst, load_sem.at[i])
        for i, (src, dst) in enumerate(((down_hbm, down_w), (gate_hbm, gate_w), (up_hbm, up_w)))
    ]
    for load in loads:
        load.start()

    lane = lax.broadcasted_iota(jnp.int32, (rows, LANES), 1)
    expert_lane = lane % experts
    first = lane < experts
    exp_logits = jnp.exp(dot(tok_ref[...], router_ref[...], NN))
    masked = jnp.where(first, exp_logits, 0.0)
    probability = exp_logits / jnp.sum(masked, axis=1, keepdims=True)
    chosen = jnp.zeros((rows, LANES), F32)
    for k in range(routes_ref.shape[1]):
        chosen = chosen + (routes_ref[:, k : k + 1] == expert_lane).astype(F32)
    selected = chosen * probability
    sel_total = jnp.sum(jnp.where(first, selected, 0.0), axis=1, keepdims=True)
    combine = selected / sel_total
    part = lane // experts
    high, mid, low = split3(combine)
    aux = jnp.where(part == 0, high, jnp.where(part == 1, mid, jnp.where(part == 2, low, 0.0)))
    tok_all[0, 0, 0, 0, :, :width] = tok_ref[...]
    tok_all[0, 0, 0, 0, :, width:] = aux.astype(BF16)
    cot_all[0, 0, 0, 0] = cot_ref[...]
    small[0] = probability
    small[1] = chosen
    small[2] = combine
    small[3] = jnp.broadcast_to(sel_total, (rows, LANES))

    pl.semaphore_wait(barrier, len(others))

    book = Book()
    sent = []
    blocks = (tok_all, cot_all)

    def copy(src, dst, to, send_key, recv_key, keep=True):
        made = pltpu.make_async_remote_copy(
            src_ref=src, dst_ref=dst,
            send_sem=send_sem.at[book("s", *send_key)], recv_sem=recv_sem.at[book(*recv_key)],
            device_id=to, device_id_type=MESH,
        )
        made.start()
        if keep:
            sent.append(made)
        return made

    def arrived(dst, *key):
        pltpu.make_async_remote_copy(
            src_ref=dst, dst_ref=dst, send_sem=send_sem.at[0], recv_sem=recv_sem.at[book(*key)],
            device_id=device(rc=1), device_id_type=MESH,
        ).wait_recv()

    later = []

    def z_send(h, from_rel, to_rel, land):
        a = blocks[h]
        return copy(
            a.at[0, from_rel, 0, 0], a.at[0, land, 0, 0], device(rz=to_rel),
            ("z", from_rel, to_rel, h), ("z", land, h), keep=False,
        )

    def middle_only(*sends):
        @pl.when(middle_chip)
        def _():
            for args in sends:
                z_send(*args)

        later.extend(sends)

    def to_x(k, h):
        a = blocks[h]
        copy(a.at[0, k, 0, 0], a.at[0, k, 0, 1], device(rx=1), ("x", k, h), ("x", k, h))

    def to_y(k, rx, h):
        a = blocks[h]
        copy(a.at[0, k, 0, rx], a.at[1, k, 0, rx], device(ry=1), ("y", k, rx, h), ("y", k, rx, h))

    def to_core(ry, k, rx, h):
        a = blocks[h]
        copy(
            a.at[ry, k, 0, rx], a.at[ry, k, 1, rx], device(rc=1), ("c", ry, k, rx, h), ("c", ry, k, rx, h)
        )

    def spread(k, h):
        to_x(k, h)
        to_core(0, k, 0, h)
        to_y(k, 0, h)

    def on_z(k, h):
        if k == 1:
            arrived(blocks[h].at[0, 1, 0, 0], "z", 1, h)
            middle_only((h, 1, 3, 2))
            spread(1, h)
        elif k == 2:
            @pl.when(middle_chip)
            def _():
                arrived(blocks[h].at[0, 3, 0, 0], "z", 3, h)
                z_send(h, 3, 1, 2)
                arrived(blocks[h].at[0, 2, 0, 0], "z", 2, h)
                z_send(h, 2, 1, 3)

            later.extend([(h, 3, 1, 2), (h, 2, 1, 3)])

            @pl.when(jnp.logical_not(middle_chip))
            def _():
                arrived(blocks[h].at[0, 2, 0, 0], "z", 2, h)

            spread(2, h)
        else:
            @pl.when(jnp.logical_not(middle_chip))
            def _():
                arrived(blocks[h].at[0, 3, 0, 0], "z", 3, h)

            spread(3, h)

    def on_x(k, h):
        arrived(blocks[h].at[0, k, 0, 1], "x", k, h)
        to_core(0, k, 1, h)
        to_y(k, 1, h)

    def on_y(k):
        for h in range(2):
            for rx in range(2):
                arrived(blocks[h].at[1, k, 0, rx], "y", k, rx, h)
                to_core(1, k, rx, h)

    def on_core(ry, k):
        for h in range(2):
            for rx in range(2):
                arrived(blocks[h].at[ry, k, 1, rx], "c", ry, k, rx, h)

    group_lane = lax.broadcasted_iota(jnp.int32, (group, LANES), 1)

    def backprop(ry, k):
        at = ry * 4 + k
        aux_rows = tok_all[ry, k, :, :, :, width:].reshape(group, LANES).astype(F32)
        scale = jnp.sum(jnp.where(group_lane % experts == me, aux_rows, 0.0), axis=1, keepdims=True)

        def step(j, comb):
            cols = pl.ds(pl.multiple_of(j * TILE, TILE), TILE)
            tok = tok_all[ry, k, :, :, :, :width].reshape(group, width)
            cot = cot_all[ry, k].reshape(group, width)
            gate = dot(tok, gate_w[:, cols], NN)
            up = dot(tok, up_w[:, cols], NN)
            raw = dot(cot, down_t[:, cols], NN)
            sigmoid = 1.0 / (1.0 + jnp.exp(-gate))
            act = gate * sigmoid
            slope = sigmoid * (1.0 + gate * (1.0 - sigmoid))
            hidden = act * up
            grad = raw * scale
            hid[at, :, cols] = (hidden * scale).astype(BF16)
            gpart[at, :, cols] = (grad * up * slope).astype(BF16)
            upart[at, :, cols] = (grad * act).astype(BF16)
            return comb + jnp.sum(hidden * raw, axis=1, keepdims=True)

        return lax.fori_loop(0, inner // TILE, step, jnp.zeros((group, 1), F32))

    def terms(k, comb):
        high, mid, low = split3(comb)
        columns = jnp.where(
            group_lane == me, high,
            jnp.where(group_lane == me + experts, mid,
                      jnp.where(group_lane == me + 2 * experts, low, 0.0)),
        )
        out_p[k, :, :, :, width:] = columns.astype(BF16).reshape(2, 2, rows, LANES)

        def step(j, carry):
            cols = pl.ds(pl.multiple_of(j * TILE, TILE), TILE)
            out = dot(hid[k], down_w[:, cols], NN)
            out_p[k, :, :, :, cols] = out.astype(BF16).reshape(2, 2, rows, TILE)
            into = dot(gpart[k], gate_t[:, cols], NN) + dot(upart[k], up_t[:, cols], NN)
            in_p[k, :, :, :, cols] = into.astype(BF16).reshape(2, 2, rows, TILE)
            return carry

        lax.fori_loop(0, width // TILE, step, 0)

    partial = ((out_p, core_o, x_o, z_o), (in_p, core_i, x_i, z_i))

    def sum_core_send(k):
        for h, (p, c, _, _) in enumerate(partial):
            copy(p.at[k, 1], c.at[k], device(rc=1), ("rc", k, h), ("rc", k, h))

    def sum_core(k):
        for h, (p, c, _, _) in enumerate(partial):
            arrived(c.at[k], "rc", k, h)
            p[k, 0] = (p[k, 0].astype(F32) + c[k].astype(F32)).astype(BF16)

    def sum_x_send(k):
        for h, (p, _, r, _) in enumerate(partial):
            copy(p.at[k, 0, 1], r.at[k], device(rx=1), ("rx", k, h), ("rx", k, h))

    def sum_x(k):
        for h, (p, _, r, q) in enumerate(partial):
            arrived(r.at[k], "rx", k, h)
            p[k, 0, 0] = (p[k, 0, 0].astype(F32) + r[k].astype(F32)).astype(BF16)
            copy(p.at[k, 0, 0], q.at[k - 1], device(rz=k), ("rz", k, h), ("rz", k, h))

    def sum_last(h):
        p, _, r, q = partial[h]
        arrived(r.at[0], "rx", 0, h)
        total = p[0, 0, 0].astype(F32) + r[0].astype(F32)
        for k in range(1, 4):
            arrived(q.at[k - 1], "rz", k, h)
            total = total + q[k - 1].astype(F32)
        return total

    def weight_grads(spans, begin, end):
        def d_step(j, carry):
            at = pl.ds(pl.multiple_of(j * TILE, TILE), TILE)
            cols = pl.ds(pl.multiple_of(dp * half + j * TILE, TILE), TILE)
            for part, acc, ref in ((gpart, acc_g, gg_ref), (upart, acc_u, ug_ref)):
                total = None
                for ry, lo, hi in spans:
                    n = (hi - lo) * group
                    term = dot(
                        tok_all[ry, lo:hi, :, :, :, cols].reshape(n, TILE),
                        part[ry * 4 + lo : ry * 4 + hi].reshape(n, inner), TN,
                    )
                    total = term if total is None else total + term
                if not begin:
                    total = total + acc[at, :]
                if end:
                    ref[at, :] = total.astype(BF16)
                else:
                    acc[at, :] = total
            return carry

        lax.fori_loop(0, half // TILE, d_step, 0)

        def f_step(j, carry):
            at = pl.ds(pl.multiple_of(j * TILE, TILE), TILE)
            cols = pl.ds(pl.multiple_of(dp * half, TILE), half)
            total = None
            for ry, lo, hi in spans:
                n = (hi - lo) * group
                term = dot(
                    hid[ry * 4 + lo : ry * 4 + hi, :, at].reshape(n, TILE),
                    cot_all[ry, lo:hi, :, :, :, cols].reshape(n, half), TN,
                )
                total = term if total is None else total + term
            if not begin:
                total = total + acc_d[at, :]
            if end:
                dg_ref[at, :] = total.astype(BF16)
            else:
                acc_d[at, :] = total
            return carry

        lax.fori_loop(0, inner // TILE, f_step, 0)

    def flip(src, dst):
        depth = src.shape[1]

        def step(j, carry):
            at = pl.ds(pl.multiple_of(j * TILE, TILE), TILE)
            if src.shape[0] > depth:
                dst[:, at] = src[at, :].T
            else:
                dst[at, :] = src[:, at].T
            return carry

        lax.fori_loop(0, max(src.shape) // TILE, step, 0)

    for h in range(2):
        z_send(h, 0, 1, 1)
        later.append((h, 0, 1, 1, True))
        middle_only((h, 0, 3, 3))
        spread(0, h)
    for load, src, dst in zip(loads, (down_w, gate_w, up_w), (down_t, gate_t, up_t)):
        load.wait()
        flip(src, dst)
    for h in range(2):
        on_z(1, h)
    for h in range(2):
        on_x(0, h)
    on_core(0, 0)
    terms(0, backprop(0, 0))
    sum_core_send(0)
    for h in range(2):
        on_z(2, h)
    for h in range(2):
        on_x(1, h)
    on_core(0, 1)
    terms(1, backprop(0, 1))
    sum_core_send(1)
    sum_core(0)
    for h in range(2):
        on_z(3, h)
    for h in range(2):
        on_x(2, h)
    on_core(0, 2)
    terms(2, backprop(0, 2))
    sum_core_send(2)
    sum_core(1)
    sum_x_send(1)
    for h in range(2):
        on_x(3, h)
    on_core(0, 3)
    terms(3, backprop(0, 3))
    sum_core_send(3)
    sum_core(2)
    sum_x_send(2)
    on_y(0)
    on_core(1, 0)
    backprop(1, 0)
    sum_core(3)
    sum_x_send(3)
    sum_x_send(0)
    sum_x(1)
    on_y(1)
    on_core(1, 1)
    backprop(1, 1)
    sum_x(2)
    weight_grads(((0, 0, 4), (1, 0, 2)), True, False)
    sum_x(3)
    on_y(2)
    on_core(1, 2)
    backprop(1, 2)

    total = sum_last(0)
    out_ref[...] = total[:, :width].astype(BF16)
    comb = total[:, width:]
    comb = comb + pltpu.roll(comb, LANES - experts, 1) + pltpu.roll(comb, LANES - 2 * experts, 1)
    comb = jnp.where(first, comb, 0.0)
    probability, chosen, combine, sel_total = small[0], small[1], small[2], small[3]
    mean = jnp.sum(combine * comb, axis=1, keepdims=True)
    sel_grad = jnp.where(first, chosen * (comb - mean) / sel_total, 0.0)
    logit_grad = probability * (sel_grad - jnp.sum(probability * sel_grad, axis=1, keepdims=True))
    high, mid, low = split3(jnp.where(first, logit_grad, 0.0))
    mine = (high + pltpu.roll(mid, experts, 1) + pltpu.roll(low, 2 * experts, 1)).astype(BF16)
    lgs[0] = mine
    for at, rel in enumerate(others):
        pltpu.make_async_remote_copy(
            src_ref=lgs.at[0], dst_ref=lgs.at[at + 1], send_sem=lg_send.at[at], recv_sem=lg_recv.at[at],
            device_id=device(*rel), device_id_type=MESH,
        ).start()
    tgrad_ref[...] = (sum_last(1) + dot(mine, router_ref[...], NT)).astype(BF16)

    on_y(3)
    on_core(1, 3)
    backprop(1, 3)
    weight_grads(((1, 2, 4),), False, True)

    for at, rel in enumerate(others):
        pltpu.make_async_remote_copy(
            src_ref=lgs.at[0], dst_ref=lgs.at[at + 1], send_sem=lg_send.at[at], recv_sem=lg_recv.at[at],
            device_id=device(*rel), device_id_type=MESH,
        ).wait()

    def r_step(j, carry):
        cols = pl.ds(pl.multiple_of(j * TILE, TILE), TILE)
        total = None
        for ry in range(2):
            term = dot(
                lgs[16 * ry : 16 * ry + 16].reshape(16 * rows, LANES),
                tok_all[ry, :, :, :, :, cols].reshape(16 * rows, TILE), TN,
            )
            total = term if total is None else total + term
        rgrad_ref[:, cols] = (
            total[:experts] + total[experts : 2 * experts] + total[2 * experts : 3 * experts]
        )
        return carry

    lax.fori_loop(0, width // TILE, r_step, 0)

    for made in sent:
        made.wait_send()

    def z_done(h, from_rel, to_rel, land):
        a = blocks[h]
        pltpu.make_async_remote_copy(
            src_ref=a.at[0, from_rel, 0, 0], dst_ref=a.at[0, land, 0, 0],
            send_sem=send_sem.at[book("s", "z", from_rel, to_rel, h)],
            recv_sem=recv_sem.at[book("z", land, h)],
            device_id=device(rz=to_rel), device_id_type=MESH,
        ).wait_send()

    for args in later:
        if len(args) == 5:
            z_done(*args[:4])

    @pl.when(middle_chip)
    def _():
        for args in later:
            if len(args) == 4:
                z_done(*args)

    assert len(book.places) <= send_sem.shape[0]


def local_fused(tokens, routes, cotangent, router_weight, gate_weight, up_weight, down_weight):
    rows, width = tokens.shape
    experts = router_weight.shape[1]
    inner = gate_weight.shape[2]
    half = width // 2
    wide = width + LANES
    vmem = lambda *shape, dtype=BF16: pltpu.VMEM(shape, dtype)
    scratch = [
        vmem(2, 4, 2, 2, rows, wide), vmem(2, 4, 2, 2, rows, width),
        vmem(width, inner), vmem(width, inner), vmem(inner, width),
        vmem(inner, width), vmem(inner, width), vmem(width, inner),
        vmem(8, 4 * rows, inner), vmem(8, 4 * rows, inner), vmem(8, 4 * rows, inner),
        vmem(4, 2, 2, rows, wide), vmem(4, 2, 2, rows, width),
        vmem(4, 2, rows, wide), vmem(4, 2, rows, width),
        vmem(4, rows, wide), vmem(4, rows, width),
        vmem(3, rows, wide), vmem(3, rows, width),
        vmem(32, rows, LANES),
        vmem(half, inner, dtype=F32), vmem(half, inner, dtype=F32), vmem(inner, half, dtype=F32),
        vmem(4, rows, LANES, dtype=F32),
        pltpu.SemaphoreType.DMA((3,)),
        pltpu.SemaphoreType.DMA((2 * COPIES,)), pltpu.SemaphoreType.DMA((2 * COPIES,)),
        pltpu.SemaphoreType.DMA((31,)), pltpu.SemaphoreType.DMA((31,)),
    ]
    in_vmem = pl.BlockSpec(memory_space=pltpu.VMEM)
    in_any = pl.BlockSpec(memory_space=pl.ANY)
    layer_out, token_grad, gate_grad, up_grad, down_grad, router_grad = pl.pallas_call(
        functools.partial(fused, experts),
        out_shape=(
            jax.ShapeDtypeStruct((rows, width), BF16),
            jax.ShapeDtypeStruct((rows, width), BF16),
            jax.ShapeDtypeStruct((half, inner), BF16),
            jax.ShapeDtypeStruct((half, inner), BF16),
            jax.ShapeDtypeStruct((inner, half), BF16),
            jax.ShapeDtypeStruct((experts, width), F32),
        ),
        in_specs=[in_vmem] * 4 + [in_any] * 3,
        out_specs=(in_vmem,) * 6,
        scratch_shapes=scratch,
        compiler_params=pltpu.CompilerParams(
            collective_id=0, has_side_effects=True, vmem_limit_bytes=62 * 2**20
        ),
    )(
        tokens, routes, cotangent, jnp.tile(router_weight, (1, LANES // experts)),
        gate_weight[0], up_weight[0], down_weight[0],
    )
    return (
        layer_out, token_grad, gate_grad[None], up_grad[None], down_grad[None], router_grad.T
    )


def silu_parts(gate_act):
    sigmoid_value = jax.nn.sigmoid(gate_act)
    act_value = gate_act * sigmoid_value
    act_slope = sigmoid_value * (1.0 + gate_act * (1.0 - sigmoid_value))
    return (act_value, act_slope)


def expert_forward(arrived, gate_weight, up_weight, down_weight):
    gate_act = jnp.einsum(
        "sjcd,jdf->sjcf", arrived, gate_weight, preferred_element_type=jnp.float32
    )
    up_act = jnp.einsum("sjcd,jdf->sjcf", arrived, up_weight, preferred_element_type=jnp.float32)
    act_value, act_slope = silu_parts(gate_act)
    hidden = (act_value * up_act).astype(jnp.bfloat16)
    expert_out = jnp.einsum(
        "sjcf,jfd->sjcd", hidden, down_weight, preferred_element_type=jnp.float32
    ).astype(jnp.bfloat16)
    return (expert_out, (up_act, act_value, act_slope, hidden))


def expert_backward(arrived_grads, stored, gate_weight, up_weight, down_weight):
    up_act, act_value, act_slope, hidden = stored
    hidden_grad = jnp.einsum(
        "sjcd,jfd->sjcf", arrived_grads, down_weight, preferred_element_type=jnp.float32
    )
    gate_part = (hidden_grad * up_act * act_slope).astype(jnp.bfloat16)
    up_part = (hidden_grad * act_value).astype(jnp.bfloat16)
    input_grad = (
        jnp.einsum("sjcf,jdf->sjcd", gate_part, gate_weight, preferred_element_type=jnp.float32)
        + jnp.einsum("sjcf,jdf->sjcd", up_part, up_weight, preferred_element_type=jnp.float32)
    ).astype(jnp.bfloat16)
    return (input_grad, gate_part, up_part)


def local_slots(tokens, routes, cotangent, router_weight, gate_weight, up_weight, down_weight):
    tok_rows, top_count = routes.shape
    model_width = tokens.shape[1]
    expert_count = router_weight.shape[1]
    local_count = gate_weight.shape[0]
    group_size = lax.axis_size("expert")
    capacity = min(tok_rows, 2 * tok_rows * top_count // expert_count)
    slot_total = expert_count * capacity
    buffer_shape = (group_size, local_count, capacity, model_width)
    logits = jnp.dot(tokens, router_weight, preferred_element_type=jnp.float32)
    exp_logits = jnp.exp(logits)
    probability = exp_logits / jnp.sum(exp_logits, axis=1, keepdims=True)
    chosen = (
        routes[:, :, None] == jnp.arange(expert_count, dtype=jnp.int32)[None, None, :]
    ).astype(jnp.int32)
    chosen_float = chosen.astype(jnp.float32)
    selected = jnp.sum(chosen_float * probability[:, None, :], axis=2)
    sel_total = jnp.sum(selected, axis=1, keepdims=True)
    combine = selected / sel_total
    per_token = jnp.sum(chosen, axis=1)
    before = jnp.tril(jnp.ones((tok_rows, tok_rows), jnp.float32), -1)
    earlier = jnp.dot(before, per_token.astype(jnp.float32)).astype(jnp.int32)
    slot_ids = jnp.sum(chosen * earlier[:, None, :], axis=2)
    flat_slot = routes * capacity + slot_ids
    match_map = (
        flat_slot[:, :, None] == jnp.arange(slot_total, dtype=jnp.int32)[None, None, :]
    ).astype(jnp.float32)
    presence = jnp.sum(match_map, axis=1)
    weight_map = jnp.sum(match_map * combine[:, :, None], axis=1)
    send_rows = (
        jnp.einsum(
            "tr,td->rd", presence.astype(jnp.bfloat16), tokens, preferred_element_type=jnp.float32
        )
        .astype(jnp.bfloat16)
        .reshape(buffer_shape)
    )
    send_grads = (
        jnp.einsum(
            "tr,td->rd", weight_map, cotangent.astype(jnp.float32), precision=lax.Precision.HIGHEST
        )
        .astype(jnp.bfloat16)
        .reshape(buffer_shape)
    )
    arrived = lax.all_to_all(send_rows, "expert", split_axis=0, concat_axis=0, tiled=True)
    expert_out, stored = expert_forward(arrived, gate_weight, up_weight, down_weight)
    returned = lax.all_to_all(expert_out, "expert", split_axis=0, concat_axis=0, tiled=True)
    arrived_grads = lax.all_to_all(send_grads, "expert", split_axis=0, concat_axis=0, tiled=True)
    input_grad, gate_part, up_part = expert_backward(
        arrived_grads, stored, gate_weight, up_weight, down_weight
    )
    returned_grads = lax.all_to_all(input_grad, "expert", split_axis=0, concat_axis=0, tiled=True)
    hidden = stored[3]
    gate_term = jnp.einsum("sjcd,sjcf->jdf", arrived, gate_part, preferred_element_type=jnp.float32)
    up_term = jnp.einsum("sjcd,sjcf->jdf", arrived, up_part, preferred_element_type=jnp.float32)
    down_term = jnp.einsum(
        "sjcf,sjcd->jfd", hidden, arrived_grads, preferred_element_type=jnp.float32
    )
    gate_sum, up_sum, down_sum = (
        lax.psum_scatter(gate_term, "dp", scatter_dimension=1, tiled=True),
        lax.psum_scatter(up_term, "dp", scatter_dimension=1, tiled=True),
        lax.psum_scatter(down_term, "dp", scatter_dimension=2, tiled=True),
    )
    gate_grad = gate_sum.astype(jnp.bfloat16)
    up_grad = up_sum.astype(jnp.bfloat16)
    down_grad = down_sum.astype(jnp.bfloat16)
    flat_index = flat_slot.reshape(-1)
    out_sel = jnp.take(returned.reshape(slot_total, model_width), flat_index, axis=0).reshape(
        tok_rows, top_count, model_width
    )
    grad_sel = jnp.take(
        returned_grads.reshape(slot_total, model_width), flat_index, axis=0
    ).reshape(tok_rows, top_count, model_width)
    layer_out = jnp.sum(combine[:, :, None] * out_sel.astype(jnp.float32), axis=1).astype(
        jnp.bfloat16
    )
    comb_grad = jnp.einsum("tkd,td->tk", out_sel, cotangent, preferred_element_type=jnp.float32)
    sel_grad = (comb_grad - jnp.sum(combine * comb_grad, axis=1, keepdims=True)) / sel_total
    prob_grad = jnp.sum(chosen_float * sel_grad[:, :, None], axis=1)
    logit_grad = probability * (prob_grad - jnp.sum(probability * prob_grad, axis=1, keepdims=True))
    router_term = jnp.einsum(
        "td,te->de", tokens.astype(jnp.float32), logit_grad, precision=lax.Precision.HIGHEST
    )
    router_grad = lax.psum(router_term, ("dp", "expert"))
    router_back = jnp.einsum(
        "te,de->td", logit_grad, router_weight.astype(jnp.float32), precision=lax.Precision.HIGHEST
    )
    token_grad = (jnp.sum(grad_sel.astype(jnp.float32), axis=1) + router_back).astype(jnp.bfloat16)
    return (layer_out, token_grad, gate_grad, up_grad, down_grad, router_grad)


def local(tokens, routes, cotangent, router_weight, gate_weight, up_weight, down_weight):
    tok_rows, top_count = routes.shape
    capacity = min(tok_rows, 2 * tok_rows * top_count // router_weight.shape[1])
    dense = (
        capacity == tok_rows
        and gate_weight.shape[0] == 1
        and router_weight.shape[1] == 16
        and lax.axis_size("dp") == 2
        and lax.axis_size("expert") == 16
    )
    plan = local_fused if dense else local_slots
    return plan(tokens, routes, cotangent, router_weight, gate_weight, up_weight, down_weight)


def solution(mesh):
    return jax.shard_map(
        local,
        mesh=mesh,
        in_specs=(
            P(("dp", "expert"), None),
            P(("dp", "expert"), None),
            P(("dp", "expert"), None),
            P(),
            P("expert", None, None),
            P("expert", None, None),
            P("expert", None, None),
        ),
        out_specs=(
            P(("dp", "expert"), None),
            P(("dp", "expert"), None),
            P("expert", "dp", None),
            P("expert", "dp", None),
            P("expert", None, "dp"),
            P(),
        ),
        check_vma=False,
    )
```

```python
import functools

import jax
import jax.numpy as jnp
from jax import lax
from jax.experimental import pallas as pl
from jax.experimental.pallas import tpu as pltpu
from jax.sharding import PartitionSpec as P

MESH = pl.DeviceIdType.MESH
NN = (((1,), (0,)), ((), ()))
NT = (((1,), (1,)), ((), ()))
TN = (((0,), (0,)), ((), ()))
F32 = jnp.float32
BF16 = jnp.bfloat16
TILE = 256
LANES = 128


def dot(a, b, dims):
    return lax.dot_general(a, b, dims, preferred_element_type=F32)


def split3(value):
    high = value.astype(BF16).astype(F32)
    middle = (value - high).astype(BF16).astype(F32)
    low = (value - high - middle).astype(BF16).astype(F32)
    return high, middle, low


class Book:
    def __init__(self):
        self.places = {}

    def __call__(self, *key):
        return self.places.setdefault(key, len(self.places))


COPIES = 110


def fused(
    experts, tok_ref, routes_ref, cot_ref, router_ref, gate_hbm, up_hbm, down_hbm,
    out_ref, tgrad_ref, gg_hbm, ug_hbm, dg_hbm, rgrad_ref,
    tok_all, cot_all, gate_w, up_w, down_w, gate_t, up_t, down_t,
    hid, gpart, upart, act_s, slope_s, hidden_s,
    out_p, in_p, comb_p, core_o, core_i, core_c, x_o, x_i, x_c, z_o, z_i, z_c,
    lgs, lgs_t, router_t, acc_g, acc_u, acc_d, gg_ref, ug_ref, dg_ref, small,
    load_sem, store_sem, send_sem, recv_sem,
):
    rows, width = tok_ref.shape
    inner = gate_w.shape[1]
    half = acc_g.shape[0]
    group = 4 * rows
    dp = lax.axis_index("dp")
    me = lax.axis_index("expert")
    z, x, core = me // 4, (me // 2) % 2, me % 2
    z_of = {0: z, 1: z + 1 - 2 * (z % 2), 2: (z + 2) % 4, 3: 3 - z}
    middle_chip = (z + 1) % 4 >= 2

    def device(ry=0, rz=0, rc=0, rx=0):
        return (
            1 - dp if ry else dp,
            z_of[rz] * 4 + (1 - x if rx else x) * 2 + (1 - core if rc else core),
        )

    barrier = pltpu.get_barrier_semaphore()
    others = [device(rc=1), device(rx=1), device(ry=1), device(rz=1), device(rz=2), device(rz=3)]
    for other in others:
        pl.semaphore_signal(barrier, inc=1, device_id=other, device_id_type=MESH)

    loads = [
        pltpu.make_async_copy(src, dst, load_sem.at[i])
        for i, (src, dst) in enumerate(((down_hbm, down_w), (gate_hbm, gate_w), (up_hbm, up_w)))
    ]
    for load in loads:
        load.start()

    lane = lax.broadcasted_iota(jnp.int32, (rows, LANES), 1)
    first = lane < experts
    for i in range(LANES // experts):
        router_t[i * experts : (i + 1) * experts, :] = router_ref[...]
    exp_logits = jnp.exp(dot(tok_ref[...], router_t[...], NT))
    masked = jnp.where(first, exp_logits, 0.0)
    probability = exp_logits / jnp.sum(masked, axis=1, keepdims=True)
    chosen = jnp.zeros((LANES, rows), F32)
    expert_row = lax.broadcasted_iota(jnp.int32, (LANES, rows), 0) % experts
    for k in range(routes_ref.shape[0]):
        chosen = chosen + (routes_ref[k : k + 1, :] == expert_row).astype(F32)
    eye = (
        lax.broadcasted_iota(jnp.int32, (rows, rows), 0)
        == lax.broadcasted_iota(jnp.int32, (rows, rows), 1)
    ).astype(F32)
    chosen = dot(eye.astype(BF16), chosen.astype(BF16), NT)
    selected = chosen * probability
    sel_total = jnp.sum(jnp.where(first, selected, 0.0), axis=1, keepdims=True)
    combine = selected / sel_total
    part = lane // experts
    high, mid, low = split3(combine)
    aux = jnp.where(part == 0, high, jnp.where(part == 1, mid, jnp.where(part == 2, low, 0.0)))
    tok_all[0, 0, 0, 0, :, :width] = tok_ref[...]
    tok_all[0, 0, 0, 0, :, width:] = aux.astype(BF16)
    cot_all[0, 0, 0, 0] = cot_ref[...]
    small[0] = probability
    small[1] = chosen
    small[2] = combine
    small[3] = jnp.broadcast_to(sel_total, (rows, LANES))

    pl.semaphore_wait(barrier, len(others))

    book = Book()
    sent = []
    blocks = (tok_all, cot_all)

    def copy(src, dst, to, send_key, recv_key, keep=True):
        made = pltpu.make_async_remote_copy(
            src_ref=src, dst_ref=dst,
            send_sem=send_sem.at[book("s", *send_key)], recv_sem=recv_sem.at[book(*recv_key)],
            device_id=to, device_id_type=MESH,
        )
        made.start()
        if keep:
            sent.append(made)
        return made

    def arrived(dst, *key):
        pltpu.make_async_remote_copy(
            src_ref=dst, dst_ref=dst, send_sem=send_sem.at[0], recv_sem=recv_sem.at[book(*key)],
            device_id=device(rc=1), device_id_type=MESH,
        ).wait_recv()

    later = []

    def z_send(h, from_rel, to_rel, land):
        a = blocks[h]
        return copy(
            a.at[0, from_rel, 0, 0], a.at[0, land, 0, 0], device(rz=to_rel),
            ("z", from_rel, to_rel, h), ("z", land, h), keep=False,
        )

    def middle_only(*sends):
        @pl.when(middle_chip)
        def _():
            for args in sends:
                z_send(*args)

        later.extend(sends)

    def to_x(k, h):
        a = blocks[h]
        copy(a.at[0, k, 0, 0], a.at[0, k, 0, 1], device(rx=1), ("x", k, h), ("x", k, h))

    def to_y(k, rx, h):
        a = blocks[h]
        copy(a.at[0, k, 0, rx], a.at[1, k, 0, rx], device(ry=1), ("y", k, rx, h), ("y", k, rx, h))

    def to_core(ry, k, rx, h):
        a = blocks[h]
        copy(
            a.at[ry, k, 0, rx], a.at[ry, k, 1, rx], device(rc=1), ("c", ry, k, rx, h), ("c", ry, k, rx, h)
        )

    def spread(k, h):
        to_x(k, h)
        to_core(0, k, 0, h)
        to_y(k, 0, h)

    def on_z(k, h):
        here = blocks[h]
        if k == 1:
            arrived(here.at[0, 1, 0, 0], "z", 1, h)

            @pl.when(middle_chip)
            def _():
                z_send(h, 1, 3, 2)
                arrived(here.at[0, 3, 0, 0], "z", 3, h)
                z_send(h, 3, 1, 2)

            later.extend([(h, 1, 3, 2), (h, 3, 1, 2)])
        elif k == 2:
            arrived(here.at[0, 2, 0, 0], "z", 2, h)
            middle_only((h, 2, 1, 3))
        else:

            @pl.when(jnp.logical_not(middle_chip))
            def _():
                arrived(here.at[0, 3, 0, 0], "z", 3, h)

        spread(k, h)

    def on_x(k, h):
        arrived(blocks[h].at[0, k, 0, 1], "x", k, h)
        to_core(0, k, 1, h)
        to_y(k, 1, h)

    def on_y(k, h):
        for rx in range(2):
            arrived(blocks[h].at[1, k, 0, rx], "y", k, rx, h)
            to_core(1, k, rx, h)

    def on_core(ry, k, h):
        for rx in range(2):
            arrived(blocks[h].at[ry, k, 1, rx], "c", ry, k, rx, h)

    group_lane = lax.broadcasted_iota(jnp.int32, (group, LANES), 1)

    def scale_of(ry, k):
        aux_rows = tok_all[ry, k, :, :, :, width:].reshape(group, LANES).astype(F32)
        return jnp.sum(jnp.where(group_lane % experts == me, aux_rows, 0.0), axis=1, keepdims=True)

    def forward(ry, k):
        scale = scale_of(ry, k)

        def step(j, carry):
            cols = pl.ds(pl.multiple_of(j * TILE, TILE), TILE)
            tok = tok_all[ry, k, :, :, :, :width].reshape(group, width)
            gate = dot(tok, gate_w[:, cols], NN)
            up = dot(tok, up_w[:, cols], NN)
            sigmoid = 1.0 / (1.0 + jnp.exp(-gate))
            act = gate * sigmoid
            hidden = act * up
            act_s[:, cols] = act
            slope_s[:, cols] = up * (sigmoid * (1.0 + gate * (1.0 - sigmoid)))
            hidden_s[:, cols] = hidden
            hid[ry * 4 + k, :, cols] = (hidden * scale).astype(BF16)
            return carry

        lax.fori_loop(0, inner // TILE, step, 0, unroll=True)

    def backward(ry, k):
        scale = scale_of(ry, k)

        def step(j, comb):
            cols = pl.ds(pl.multiple_of(j * TILE, TILE), TILE)
            raw = dot(cot_all[ry, k].reshape(group, width), down_t[:, cols], NN)
            grad = raw * scale
            gpart[ry * 4 + k, :, cols] = (grad * slope_s[:, cols]).astype(BF16)
            upart[ry * 4 + k, :, cols] = (grad * act_s[:, cols]).astype(BF16)
            return comb + jnp.sum(hidden_s[:, cols] * raw, axis=1, keepdims=True)

        comb = lax.fori_loop(0, inner // TILE, step, jnp.zeros((group, 1), F32), unroll=True)
        if ry == 0:
            high, mid, low = split3(comb)
            columns = jnp.where(
                group_lane == me, high,
                jnp.where(group_lane == me + experts, mid,
                          jnp.where(group_lane == me + 2 * experts, low, 0.0)),
            )
            comb_p[k] = columns.astype(BF16).reshape(2, 2, rows, LANES)

    def out_terms(k):
        def step(j, carry):
            cols = pl.ds(pl.multiple_of(j * TILE, TILE), TILE)
            out = dot(hid[k], down_w[:, cols], NN)
            out_p[k, :, :, :, cols] = out.astype(BF16).reshape(2, 2, rows, TILE)
            return carry

        lax.fori_loop(0, width // TILE, step, 0, unroll=True)
        core_send(k, 0)

    def in_terms(k):
        def step(j, carry):
            cols = pl.ds(pl.multiple_of(j * TILE, TILE), TILE)
            into = dot(gpart[k], gate_t[:, cols], NN) + dot(upart[k], up_t[:, cols], NN)
            in_p[k, :, :, :, cols] = into.astype(BF16).reshape(2, 2, rows, TILE)
            return carry

        lax.fori_loop(0, width // TILE, step, 0, unroll=True)
        core_send(k, 1)

    partial = ((out_p, core_o, x_o, z_o), (in_p, core_i, x_i, z_i))

    def core_send(k, h):
        p, c, _, _ = partial[h]
        copy(p.at[k, 1], c.at[k], device(rc=1), ("rc", k, h), ("rc", k, h))

    def core_sum(k, h):
        p, c, r, _ = partial[h]
        arrived(c.at[k], "rc", k, h)
        p[k, 0] = (p[k, 0].astype(F32) + c[k].astype(F32)).astype(BF16)
        copy(p.at[k, 0, 1], r.at[k], device(rx=1), ("rx", k, h), ("rx", k, h))

    def x_sum(k, h):
        p, _, r, q = partial[h]
        arrived(r.at[k], "rx", k, h)
        p[k, 0, 0] = (p[k, 0, 0].astype(F32) + r[k].astype(F32)).astype(BF16)
        copy(p.at[k, 0, 0], q.at[k - 1], device(rz=k), ("rz", k, h), ("rz", k, h))

    def last_sum(h):
        p, _, r, q = partial[h]
        arrived(r.at[0], "rx", 0, h)
        total = p[0, 0, 0].astype(F32) + r[0].astype(F32)
        for k in range(1, 4):
            arrived(q.at[k - 1], "rz", k, h)
            total = total + q[k - 1].astype(F32)
        return total

    def comb_send():
        copy(comb_p.at[:, 1], core_c, device(rc=1), ("cc",), ("cc",))

    def comb_core():
        arrived(core_c, "cc")
        comb_p[:, 0] = (comb_p[:, 0].astype(F32) + core_c[...].astype(F32)).astype(BF16)
        copy(comb_p.at[:, 0, 1], x_c, device(rx=1), ("cx",), ("cx",))

    def comb_x():
        arrived(x_c, "cx")
        comb_p[:, 0, 0] = (comb_p[:, 0, 0].astype(F32) + x_c[...].astype(F32)).astype(BF16)
        for k in range(1, 4):
            copy(comb_p.at[k, 0, 0], z_c.at[k - 1], device(rz=k), ("cz", k), ("cz", k))

    def comb_last():
        total = comb_p[0, 0, 0].astype(F32)
        for k in range(1, 4):
            arrived(z_c.at[k - 1], "cz", k)
            total = total + z_c[k - 1].astype(F32)
        return total

    def width_grads(spans, begin, end):
        def d_step(j, carry):
            at = pl.ds(pl.multiple_of(j * TILE, TILE), TILE)
            cols = pl.ds(pl.multiple_of(dp * half + j * TILE, TILE), TILE)
            for part, acc, ref in ((gpart, acc_g, gg_ref), (upart, acc_u, ug_ref)):
                total = None
                for ry, lo, hi in spans:
                    n = (hi - lo) * group
                    term = dot(
                        tok_all[ry, lo:hi, :, :, :, cols].reshape(n, TILE),
                        part[ry * 4 + lo : ry * 4 + hi].reshape(n, inner), TN,
                    )
                    total = term if total is None else total + term
                if not begin:
                    total = total + acc[at, :]
                if end:
                    ref[at, :] = total.astype(BF16)
                else:
                    acc[at, :] = total
            return carry

        lax.fori_loop(0, half // TILE, d_step, 0, unroll=True)

    def inner_grads(spans, begin, end):
        def f_step(j, carry):
            at = pl.ds(pl.multiple_of(j * TILE, TILE), TILE)
            cols = pl.ds(pl.multiple_of(dp * half, TILE), half)
            total = None
            for ry, lo, hi in spans:
                n = (hi - lo) * group
                term = dot(
                    hid[ry * 4 + lo : ry * 4 + hi, :, at].reshape(n, TILE),
                    cot_all[ry, lo:hi, :, :, :, cols].reshape(n, half), TN,
                )
                total = term if total is None else total + term
            if not begin:
                total = total + acc_d[at, :]
            if end:
                dg_ref[at, :] = total.astype(BF16)
            else:
                acc_d[at, :] = total
            return carry

        lax.fori_loop(0, inner // TILE, f_step, 0, unroll=True)

    def flip(src, dst):
        depth = src.shape[1]

        def step(j, carry):
            at = pl.ds(pl.multiple_of(j * TILE, TILE), TILE)
            if src.shape[0] > depth:
                dst[:, at] = src[at, :].T
            else:
                dst[at, :] = src[:, at].T
            return carry

        lax.fori_loop(0, max(src.shape) // TILE, step, 0, unroll=True)

    for h in range(2):
        z_send(h, 0, 1, 1)
        later.append((h, 0, 1, 1, True))
        middle_only((h, 0, 3, 3))
        spread(0, h)
    for load, src, dst in zip(loads, (down_w, gate_w, up_w), (down_t, gate_t, up_t)):
        load.wait()
        flip(src, dst)
    TOK, COT, OUT, IN = 0, 1, 0, 1
    for k in range(4):
        for h in (TOK, COT):
            if k < 3:
                on_z(k + 1, h)
            on_x(k, h)
            on_core(0, k, h)
            if h == TOK:
                forward(0, k)
                if k == 3:
                    core_sum(2, IN)
                out_terms(k)
            else:
                backward(0, k)
                if k == 2:
                    core_sum(2, OUT)
                if k == 3:
                    core_sum(3, OUT)
                    x_sum(2, OUT)
                in_terms(k)
    comb_send()
    for h in (TOK, COT):
        on_y(0, h)
    core_sum(3, IN)
    x_sum(3, OUT)
    x_sum(2, IN)
    comb_core()
    core_sum(1, OUT)
    core_sum(1, IN)
    core_sum(0, OUT)
    core_sum(0, IN)
    on_core(1, 0, TOK)
    forward(1, 0)
    on_core(1, 0, COT)
    backward(1, 0)
    comb_x()
    x_sum(3, IN)
    for h in (TOK, COT):
        on_y(1, h)
    on_core(1, 1, TOK)
    forward(1, 1)
    on_core(1, 1, COT)
    backward(1, 1)
    width_grads(((0, 0, 4), (1, 0, 2)), True, False)
    x_sum(1, OUT)
    x_sum(1, IN)
    inner_grads(((0, 0, 4), (1, 0, 2)), True, False)
    for h in (TOK, COT):
        on_y(2, h)
    on_core(1, 2, TOK)
    forward(1, 2)
    on_core(1, 2, COT)
    backward(1, 2)

    comb = comb_last()
    comb = comb + pltpu.roll(comb, LANES - experts, 1) + pltpu.roll(comb, LANES - 2 * experts, 1)
    comb = jnp.where(first, comb, 0.0)
    probability, chosen, combine, sel_total = small[0], small[1], small[2], small[3]
    mean = jnp.sum(combine * comb, axis=1, keepdims=True)
    sel_grad = jnp.where(first, chosen * (comb - mean) / sel_total, 0.0)
    logit_grad = probability * (sel_grad - jnp.sum(probability * sel_grad, axis=1, keepdims=True))
    high, mid, low = split3(jnp.where(first, logit_grad, 0.0))
    mine = (high + pltpu.roll(mid, experts, 1) + pltpu.roll(low, 2 * experts, 1)).astype(BF16)
    lgs[0, 0, 0, 0] = mine
    hops = (
        (lgs.at[0, 0, 0, 0], lgs.at[0, 0, 1, 0], device(rc=1)),
        (lgs.at[0, 0, :, 0], lgs.at[0, 0, :, 1], device(rx=1)),
        (lgs.at[0, 0], lgs.at[0, 1], device(rz=1)),
        (lgs.at[0, 0], lgs.at[0, 2], device(rz=2)),
        (lgs.at[0, 0], lgs.at[0, 3], device(rz=3)),
        (lgs.at[0], lgs.at[1], device(ry=1)),
    )

    def hop(*steps):
        for i in steps:
            src, dst, to = hops[i]
            copy(src, dst, to, ("l", i), ("l", i))

    def hopped(*steps):
        for i in steps:
            arrived(hops[i][1], "l", i)

    hop(0)
    out_ref[...] = last_sum(OUT).astype(BF16)
    on_y(3, TOK)
    on_core(1, 3, TOK)
    forward(1, 3)
    hopped(0)
    hop(1)
    on_y(3, COT)
    hopped(1)
    hop(2, 3, 4)
    on_core(1, 3, COT)
    backward(1, 3)
    stores = [
        pltpu.make_async_copy(src, dst, store_sem.at[i])
        for i, (src, dst) in enumerate(((gg_ref, gg_hbm), (ug_ref, ug_hbm), (dg_ref, dg_hbm)))
    ]
    width_grads(((1, 2, 4),), False, True)
    stores[0].start()
    stores[1].start()
    hopped(2, 3, 4)
    hop(5)
    inner_grads(((1, 2, 4),), False, True)
    stores[2].start()
    tgrad_ref[...] = (last_sum(IN) + dot(mine, router_t[...], NN)).astype(BF16)
    hopped(5)
    lgs_t[...] = lgs[...].reshape(32 * rows, LANES).astype(F32).T.astype(BF16)

    def r_step(j, carry):
        cols = pl.ds(pl.multiple_of(j * TILE, TILE), TILE)
        total = dot(
            lgs_t[: 3 * experts, :], tok_all[:, :, :, :, :, cols].reshape(32 * rows, TILE), NN
        )
        rgrad_ref[:, cols] = (
            total[:experts] + total[experts : 2 * experts] + total[2 * experts : 3 * experts]
        )
        return carry

    lax.fori_loop(0, width // TILE, r_step, 0, unroll=True)

    for store in stores:
        store.wait()
    for made in sent:
        made.wait_send()

    def z_done(h, from_rel, to_rel, land):
        a = blocks[h]
        pltpu.make_async_remote_copy(
            src_ref=a.at[0, from_rel, 0, 0], dst_ref=a.at[0, land, 0, 0],
            send_sem=send_sem.at[book("s", "z", from_rel, to_rel, h)],
            recv_sem=recv_sem.at[book("z", land, h)],
            device_id=device(rz=to_rel), device_id_type=MESH,
        ).wait_send()

    for args in later:
        if len(args) == 5:
            z_done(*args[:4])

    @pl.when(middle_chip)
    def _():
        for args in later:
            if len(args) == 4:
                z_done(*args)

    assert len(book.places) <= send_sem.shape[0]


def hand_over(arrays):
    n = len(arrays)
    pieces = [4 if a.shape[0] >= 128 else 2 for a in arrays]

    def kernel(*refs):
        sources, targets, held = refs[:n], refs[n : 2 * n], refs[2 * n : 3 * n]
        in_sem, out_sem = refs[3 * n :]
        ins, outs = [], []
        for i in range(n):
            step = arrays[i].shape[0] // pieces[i]
            for j in range(pieces[i]):
                at = pl.ds(j * step, step)
                ins.append(pltpu.make_async_copy(sources[i].at[at], held[i].at[at], in_sem.at[i, j]))
                outs.append(pltpu.make_async_copy(held[i].at[at], targets[i].at[at], out_sem.at[i, j]))
        for made in ins:
            made.start()
        for before, made in zip(ins, outs):
            before.wait()
            made.start()
        for made in outs:
            made.wait()

    return pl.pallas_call(
        kernel,
        out_shape=tuple(jax.ShapeDtypeStruct(a.shape, a.dtype) for a in arrays),
        in_specs=[pl.BlockSpec(memory_space=pl.ANY)] * n,
        out_specs=(pl.BlockSpec(memory_space=pl.ANY),) * n,
        scratch_shapes=[pltpu.VMEM(a.shape, a.dtype) for a in arrays]
        + [pltpu.SemaphoreType.DMA((n, 4)), pltpu.SemaphoreType.DMA((n, 4))],
        compiler_params=pltpu.CompilerParams(vmem_limit_bytes=60 * 2**20),
    )(*arrays)


def local_fused(tokens, routes, cotangent, router_weight, gate_weight, up_weight, down_weight):
    rows, width = tokens.shape
    experts = router_weight.shape[1]
    inner = gate_weight.shape[2]
    half = width // 2
    wide = width + LANES
    vmem = lambda *shape, dtype=BF16: pltpu.VMEM(shape, dtype)
    scratch = [
        vmem(2, 4, 2, 2, rows, wide), vmem(2, 4, 2, 2, rows, width),
        vmem(width, inner), vmem(width, inner), vmem(inner, width),
        vmem(inner, width), vmem(inner, width), vmem(width, inner),
        vmem(8, 4 * rows, inner), vmem(8, 4 * rows, inner), vmem(8, 4 * rows, inner),
        vmem(4 * rows, inner, dtype=F32), vmem(4 * rows, inner, dtype=F32),
        vmem(4 * rows, inner, dtype=F32),
        vmem(4, 2, 2, rows, width), vmem(4, 2, 2, rows, width), vmem(4, 2, 2, rows, LANES),
        vmem(4, 2, rows, width), vmem(4, 2, rows, width), vmem(4, 2, rows, LANES),
        vmem(4, rows, width), vmem(4, rows, width), vmem(4, rows, LANES),
        vmem(3, rows, width), vmem(3, rows, width), vmem(3, rows, LANES),
        vmem(2, 4, 2, 2, rows, LANES), vmem(LANES, 32 * rows), vmem(LANES, width),
        vmem(half, inner, dtype=F32), vmem(half, inner, dtype=F32), vmem(inner, half, dtype=F32),
        vmem(half, inner), vmem(half, inner), vmem(inner, half),
        vmem(4, rows, LANES, dtype=F32),
        pltpu.SemaphoreType.DMA((3,)), pltpu.SemaphoreType.DMA((3,)),
        pltpu.SemaphoreType.DMA((2 * COPIES,)), pltpu.SemaphoreType.DMA((2 * COPIES,)),
    ]
    in_vmem = pl.BlockSpec(memory_space=pltpu.VMEM)
    in_any = pl.BlockSpec(memory_space=pl.ANY)
    results = pl.pallas_call(
        functools.partial(fused, experts),
        out_shape=(
            jax.ShapeDtypeStruct((rows, width), BF16),
            jax.ShapeDtypeStruct((rows, width), BF16),
            jax.ShapeDtypeStruct((half, inner), BF16),
            jax.ShapeDtypeStruct((half, inner), BF16),
            jax.ShapeDtypeStruct((inner, half), BF16),
            jax.ShapeDtypeStruct((experts, width), F32),
        ),
        in_specs=[in_vmem] * 4 + [in_any] * 3,
        out_specs=(in_vmem, in_vmem, in_any, in_any, in_any, in_vmem),
        scratch_shapes=scratch,
        compiler_params=pltpu.CompilerParams(
            collective_id=0, has_side_effects=True, vmem_limit_bytes=62 * 2**20
        ),
    )(
        tokens, routes.T, cotangent, router_weight.T, gate_weight[0], up_weight[0], down_weight[0]
    )
    layer_out, token_grad, gate_grad, up_grad, down_grad, router_grad = hand_over(results)
    return (
        layer_out, token_grad, gate_grad[None], up_grad[None], down_grad[None], router_grad.T
    )


def silu_parts(gate_act):
    sigmoid_value = jax.nn.sigmoid(gate_act)
    act_value = gate_act * sigmoid_value
    act_slope = sigmoid_value * (1.0 + gate_act * (1.0 - sigmoid_value))
    return (act_value, act_slope)


def expert_forward(arrived, gate_weight, up_weight, down_weight):
    gate_act = jnp.einsum(
        "sjcd,jdf->sjcf", arrived, gate_weight, preferred_element_type=jnp.float32
    )
    up_act = jnp.einsum("sjcd,jdf->sjcf", arrived, up_weight, preferred_element_type=jnp.float32)
    act_value, act_slope = silu_parts(gate_act)
    hidden = (act_value * up_act).astype(jnp.bfloat16)
    expert_out = jnp.einsum(
        "sjcf,jfd->sjcd", hidden, down_weight, preferred_element_type=jnp.float32
    ).astype(jnp.bfloat16)
    return (expert_out, (up_act, act_value, act_slope, hidden))


def expert_backward(arrived_grads, stored, gate_weight, up_weight, down_weight):
    up_act, act_value, act_slope, hidden = stored
    hidden_grad = jnp.einsum(
        "sjcd,jfd->sjcf", arrived_grads, down_weight, preferred_element_type=jnp.float32
    )
    gate_part = (hidden_grad * up_act * act_slope).astype(jnp.bfloat16)
    up_part = (hidden_grad * act_value).astype(jnp.bfloat16)
    input_grad = (
        jnp.einsum("sjcf,jdf->sjcd", gate_part, gate_weight, preferred_element_type=jnp.float32)
        + jnp.einsum("sjcf,jdf->sjcd", up_part, up_weight, preferred_element_type=jnp.float32)
    ).astype(jnp.bfloat16)
    return (input_grad, gate_part, up_part)


def local_slots(tokens, routes, cotangent, router_weight, gate_weight, up_weight, down_weight):
    tok_rows, top_count = routes.shape
    model_width = tokens.shape[1]
    expert_count = router_weight.shape[1]
    local_count = gate_weight.shape[0]
    group_size = lax.axis_size("expert")
    capacity = min(tok_rows, 2 * tok_rows * top_count // expert_count)
    slot_total = expert_count * capacity
    buffer_shape = (group_size, local_count, capacity, model_width)
    logits = jnp.dot(tokens, router_weight, preferred_element_type=jnp.float32)
    exp_logits = jnp.exp(logits)
    probability = exp_logits / jnp.sum(exp_logits, axis=1, keepdims=True)
    chosen = (
        routes[:, :, None] == jnp.arange(expert_count, dtype=jnp.int32)[None, None, :]
    ).astype(jnp.int32)
    chosen_float = chosen.astype(jnp.float32)
    selected = jnp.sum(chosen_float * probability[:, None, :], axis=2)
    sel_total = jnp.sum(selected, axis=1, keepdims=True)
    combine = selected / sel_total
    per_token = jnp.sum(chosen, axis=1)
    before = jnp.tril(jnp.ones((tok_rows, tok_rows), jnp.float32), -1)
    earlier = jnp.dot(before, per_token.astype(jnp.float32)).astype(jnp.int32)
    slot_ids = jnp.sum(chosen * earlier[:, None, :], axis=2)
    flat_slot = routes * capacity + slot_ids
    match_map = (
        flat_slot[:, :, None] == jnp.arange(slot_total, dtype=jnp.int32)[None, None, :]
    ).astype(jnp.float32)
    presence = jnp.sum(match_map, axis=1)
    weight_map = jnp.sum(match_map * combine[:, :, None], axis=1)
    send_rows = (
        jnp.einsum(
            "tr,td->rd", presence.astype(jnp.bfloat16), tokens, preferred_element_type=jnp.float32
        )
        .astype(jnp.bfloat16)
        .reshape(buffer_shape)
    )
    send_grads = (
        jnp.einsum(
            "tr,td->rd", weight_map, cotangent.astype(jnp.float32), precision=lax.Precision.HIGHEST
        )
        .astype(jnp.bfloat16)
        .reshape(buffer_shape)
    )
    arrived = lax.all_to_all(send_rows, "expert", split_axis=0, concat_axis=0, tiled=True)
    expert_out, stored = expert_forward(arrived, gate_weight, up_weight, down_weight)
    returned = lax.all_to_all(expert_out, "expert", split_axis=0, concat_axis=0, tiled=True)
    arrived_grads = lax.all_to_all(send_grads, "expert", split_axis=0, concat_axis=0, tiled=True)
    input_grad, gate_part, up_part = expert_backward(
        arrived_grads, stored, gate_weight, up_weight, down_weight
    )
    returned_grads = lax.all_to_all(input_grad, "expert", split_axis=0, concat_axis=0, tiled=True)
    hidden = stored[3]
    gate_term = jnp.einsum("sjcd,sjcf->jdf", arrived, gate_part, preferred_element_type=jnp.float32)
    up_term = jnp.einsum("sjcd,sjcf->jdf", arrived, up_part, preferred_element_type=jnp.float32)
    down_term = jnp.einsum(
        "sjcf,sjcd->jfd", hidden, arrived_grads, preferred_element_type=jnp.float32
    )
    gate_sum, up_sum, down_sum = (
        lax.psum_scatter(gate_term, "dp", scatter_dimension=1, tiled=True),
        lax.psum_scatter(up_term, "dp", scatter_dimension=1, tiled=True),
        lax.psum_scatter(down_term, "dp", scatter_dimension=2, tiled=True),
    )
    gate_grad = gate_sum.astype(jnp.bfloat16)
    up_grad = up_sum.astype(jnp.bfloat16)
    down_grad = down_sum.astype(jnp.bfloat16)
    flat_index = flat_slot.reshape(-1)
    out_sel = jnp.take(returned.reshape(slot_total, model_width), flat_index, axis=0).reshape(
        tok_rows, top_count, model_width
    )
    grad_sel = jnp.take(
        returned_grads.reshape(slot_total, model_width), flat_index, axis=0
    ).reshape(tok_rows, top_count, model_width)
    layer_out = jnp.sum(combine[:, :, None] * out_sel.astype(jnp.float32), axis=1).astype(
        jnp.bfloat16
    )
    comb_grad = jnp.einsum("tkd,td->tk", out_sel, cotangent, preferred_element_type=jnp.float32)
    sel_grad = (comb_grad - jnp.sum(combine * comb_grad, axis=1, keepdims=True)) / sel_total
    prob_grad = jnp.sum(chosen_float * sel_grad[:, :, None], axis=1)
    logit_grad = probability * (prob_grad - jnp.sum(probability * prob_grad, axis=1, keepdims=True))
    router_term = jnp.einsum(
        "td,te->de", tokens.astype(jnp.float32), logit_grad, precision=lax.Precision.HIGHEST
    )
    router_grad = lax.psum(router_term, ("dp", "expert"))
    router_back = jnp.einsum(
        "te,de->td", logit_grad, router_weight.astype(jnp.float32), precision=lax.Precision.HIGHEST
    )
    token_grad = (jnp.sum(grad_sel.astype(jnp.float32), axis=1) + router_back).astype(jnp.bfloat16)
    return (layer_out, token_grad, gate_grad, up_grad, down_grad, router_grad)


def local(tokens, routes, cotangent, router_weight, gate_weight, up_weight, down_weight):
    tok_rows, top_count = routes.shape
    capacity = min(tok_rows, 2 * tok_rows * top_count // router_weight.shape[1])
    dense = (
        capacity == tok_rows
        and gate_weight.shape[0] == 1
        and router_weight.shape[1] == 16
        and lax.axis_size("dp") == 2
        and lax.axis_size("expert") == 16
    )
    plan = local_fused if dense else local_slots
    return plan(tokens, routes, cotangent, router_weight, gate_weight, up_weight, down_weight)


def solution(mesh):
    return jax.shard_map(
        local,
        mesh=mesh,
        in_specs=(
            P(("dp", "expert"), None),
            P(("dp", "expert"), None),
            P(("dp", "expert"), None),
            P(),
            P("expert", None, None),
            P("expert", None, None),
            P("expert", None, None),
        ),
        out_specs=(
            P(("dp", "expert"), None),
            P(("dp", "expert"), None),
            P("expert", "dp", None),
            P("expert", "dp", None),
            P("expert", None, "dp"),
            P(),
        ),
        check_vma=False,
    )
```

```python
import functools

import jax
import jax.numpy as jnp
from jax import lax
from jax.experimental import pallas as pl
from jax.experimental.pallas import tpu as pltpu
from jax.sharding import PartitionSpec as P

MESH = pl.DeviceIdType.MESH
NN = (((1,), (0,)), ((), ()))
NT = (((1,), (1,)), ((), ()))
TN = (((0,), (0,)), ((), ()))
F32 = jnp.float32
BF16 = jnp.bfloat16
TILE = 256
LANES = 128


def dot(a, b, dims):
    return lax.dot_general(a, b, dims, preferred_element_type=F32)


def split3(value):
    high = value.astype(BF16).astype(F32)
    middle = (value - high).astype(BF16).astype(F32)
    low = (value - high - middle).astype(BF16).astype(F32)
    return high, middle, low


class Book:
    def __init__(self):
        self.places = {}

    def __call__(self, *key):
        return self.places.setdefault(key, len(self.places))


COPIES = 110


def fused(
    experts, tok_ref, routes_ref, cot_ref, router_ref, gate_hbm, up_hbm, down_hbm,
    out_ref, tgrad_ref, gg_hbm, ug_hbm, dg_hbm, rgrad_ref,
    tok_all, cot_all, gate_w, up_w, down_w, gate_t, up_t, down_t,
    hid, gpart, upart, act_s, slope_s, hidden_s,
    out_p, in_p, core_o, core_i, x_o, x_i, z_o, z_i,
    combs, comb_s, lgs_t, router_t, acc_g, acc_u, acc_d, gg_ref, ug_ref, dg_ref,
    load_sem, store_sem, send_sem, recv_sem,
):
    rows, width = tok_ref.shape
    inner = gate_w.shape[1]
    half = acc_g.shape[0]
    group = 4 * rows
    dp = lax.axis_index("dp")
    me = lax.axis_index("expert")
    z, x, core = me // 4, (me // 2) % 2, me % 2
    z_of = {0: z, 1: z + 1 - 2 * (z % 2), 2: (z + 2) % 4, 3: 3 - z}
    middle_chip = (z + 1) % 4 >= 2

    def device(ry=0, rz=0, rc=0, rx=0):
        return (
            1 - dp if ry else dp,
            z_of[rz] * 4 + (1 - x if rx else x) * 2 + (1 - core if rc else core),
        )

    barrier = pltpu.get_barrier_semaphore()
    others = [device(rc=1), device(rx=1), device(ry=1), device(rz=1), device(rz=2), device(rz=3)]
    for other in others:
        pl.semaphore_signal(barrier, inc=1, device_id=other, device_id_type=MESH)

    loads = [
        pltpu.make_async_copy(src, dst, load_sem.at[i])
        for i, (src, dst) in enumerate(((down_hbm, down_w), (gate_hbm, gate_w), (up_hbm, up_w)))
    ]
    for load in loads:
        load.start()

    lane = lax.broadcasted_iota(jnp.int32, (rows, LANES), 1)
    first = lane < experts
    for i in range(LANES // experts):
        router_t[i * experts : (i + 1) * experts, :] = router_ref[...]
    exp_logits = jnp.exp(dot(tok_ref[...], router_t[...], NT))
    masked = jnp.where(first, exp_logits, 0.0)
    probability = exp_logits / jnp.sum(masked, axis=1, keepdims=True)
    chosen = jnp.zeros((LANES, rows), F32)
    expert_row = lax.broadcasted_iota(jnp.int32, (LANES, rows), 0) % experts
    for k in range(routes_ref.shape[0]):
        chosen = chosen + (routes_ref[k : k + 1, :] == expert_row).astype(F32)
    eye = (
        lax.broadcasted_iota(jnp.int32, (rows, rows), 0)
        == lax.broadcasted_iota(jnp.int32, (rows, rows), 1)
    ).astype(F32)
    chosen = dot(eye.astype(BF16), chosen.astype(BF16), NT)
    selected = chosen * probability
    sel_total = jnp.sum(jnp.where(first, selected, 0.0), axis=1, keepdims=True)
    combine = selected / sel_total
    part = lane // experts
    aux = jnp.zeros((rows, LANES), F32)
    for i, term in enumerate(split3(combine) + split3(probability)):
        aux = jnp.where(part == i, term, aux)
    tok_all[0, 0, 0, 0, :, :width] = tok_ref[...]
    tok_all[0, 0, 0, 0, :, width:] = aux.astype(BF16)
    cot_all[0, 0, 0, 0] = cot_ref[...]

    pl.semaphore_wait(barrier, len(others))

    book = Book()
    sent = []
    blocks = (tok_all, cot_all)

    def copy(src, dst, to, send_key, recv_key, keep=True):
        made = pltpu.make_async_remote_copy(
            src_ref=src, dst_ref=dst,
            send_sem=send_sem.at[book("s", *send_key)], recv_sem=recv_sem.at[book(*recv_key)],
            device_id=to, device_id_type=MESH,
        )
        made.start()
        if keep:
            sent.append(made)
        return made

    def arrived(dst, *key):
        pltpu.make_async_remote_copy(
            src_ref=dst, dst_ref=dst, send_sem=send_sem.at[0], recv_sem=recv_sem.at[book(*key)],
            device_id=device(rc=1), device_id_type=MESH,
        ).wait_recv()

    later = []

    def z_send(h, from_rel, to_rel, land):
        a = blocks[h]
        return copy(
            a.at[0, from_rel, 0, 0], a.at[0, land, 0, 0], device(rz=to_rel),
            ("z", from_rel, to_rel, h), ("z", land, h), keep=False,
        )

    def middle_only(*sends):
        @pl.when(middle_chip)
        def _():
            for args in sends:
                z_send(*args)

        later.extend(sends)

    def to_x(k, h):
        a = blocks[h]
        copy(a.at[0, k, 0, 0], a.at[0, k, 0, 1], device(rx=1), ("x", k, h), ("x", k, h))

    def to_y(k, rx, h):
        a = blocks[h]
        copy(a.at[0, k, 0, rx], a.at[1, k, 0, rx], device(ry=1), ("y", k, rx, h), ("y", k, rx, h))

    def to_core(ry, k, rx, h):
        a = blocks[h]
        copy(
            a.at[ry, k, 0, rx], a.at[ry, k, 1, rx], device(rc=1), ("c", ry, k, rx, h), ("c", ry, k, rx, h)
        )

    def spread(k, h):
        to_x(k, h)
        to_core(0, k, 0, h)
        if k != 1:
            to_y(k, 0, h)

    def on_z(k, h):
        here = blocks[h]
        if k == 1:
            arrived(here.at[0, 1, 0, 0], "z", 1, h)

            @pl.when(middle_chip)
            def _():
                z_send(h, 1, 3, 2)
                arrived(here.at[0, 3, 0, 0], "z", 3, h)
                z_send(h, 3, 1, 2)

            later.extend([(h, 1, 3, 2), (h, 3, 1, 2)])
        elif k == 2:
            arrived(here.at[0, 2, 0, 0], "z", 2, h)
            middle_only((h, 2, 1, 3))
        else:

            @pl.when(jnp.logical_not(middle_chip))
            def _():
                arrived(here.at[0, 3, 0, 0], "z", 3, h)

        spread(k, h)

    def on_x(k, h):
        arrived(blocks[h].at[0, k, 0, 1], "x", k, h)
        to_core(0, k, 1, h)
        to_y(k, 1, h)

    def on_y(k, rx, h):
        a = blocks[h]
        arrived(a.at[1, k, 0, rx], "y", k, rx, h)
        to_core(1, k, rx, h)
        if (k, rx) == (0, 0):
            copy(a.at[1, 0, 0, 0], a.at[1, 1, 0, 0], device(rz=1), ("yz", h), ("y", 1, 0, h))

    def on_core(ry, k, h):
        for rx in range(2):
            arrived(blocks[h].at[ry, k, 1, rx], "c", ry, k, rx, h)

    group_lane = lax.broadcasted_iota(jnp.int32, (group, LANES), 1)

    diagonal = group_lane == lax.broadcasted_iota(jnp.int32, (group, LANES), 0)
    comb_row = lax.broadcasted_iota(jnp.int32, (8, LANES), 0)

    def swap_lanes(value):
        even = (lax.broadcasted_iota(jnp.int32, value.shape, 1) // rows) % 2 == 0
        swapped = jnp.where(even, pltpu.roll(value, LANES - rows, 1), pltpu.roll(value, rows, 1))
        value = jnp.where(x == 1, swapped, value)
        return jnp.where(core == 1, pltpu.roll(value, 2 * rows, 1), value)

    def scale_of(ry, k):
        aux_rows = tok_all[ry, k, :, :, :, width:].reshape(group, LANES).astype(F32)
        return jnp.sum(jnp.where((group_lane % experts == me) & (group_lane < 3 * experts), aux_rows, 0.0), axis=1, keepdims=True)

    def forward(ry, k):
        scale = scale_of(ry, k)

        def step(j, carry):
            cols = pl.ds(pl.multiple_of(j * TILE, TILE), TILE)
            tok = tok_all[ry, k, :, :, :, :width].reshape(group, width)
            gate = dot(tok, gate_w[:, cols], NN)
            up = dot(tok, up_w[:, cols], NN)
            sigmoid = 1.0 / (1.0 + jnp.exp(-gate))
            act = gate * sigmoid
            hidden = act * up
            act_s[:, cols] = act
            slope_s[:, cols] = up * (sigmoid * (1.0 + gate * (1.0 - sigmoid)))
            hidden_s[:, cols] = hidden
            hid[ry * 4 + k, :, cols] = (hidden * scale).astype(BF16)
            return carry

        lax.fori_loop(0, inner // TILE, step, 0, unroll=True)

    def backward(ry, k):
        scale = scale_of(ry, k)

        def step(j, comb):
            cols = pl.ds(pl.multiple_of(j * TILE, TILE), TILE)
            raw = dot(cot_all[ry, k].reshape(group, width), down_t[:, cols], NN)
            grad = raw * scale
            gpart[ry * 4 + k, :, cols] = (grad * slope_s[:, cols]).astype(BF16)
            upart[ry * 4 + k, :, cols] = (grad * act_s[:, cols]).astype(BF16)
            return comb + jnp.sum(hidden_s[:, cols] * raw, axis=1, keepdims=True)

        comb = lax.fori_loop(0, inner // TILE, step, jnp.zeros((group, 1), F32), unroll=True)
        if ry == 0:
            row = jnp.sum(jnp.where(diagonal, comb, 0.0), axis=0, keepdims=True)
            here = jnp.where(comb_row == z_of[k], swap_lanes(row), 0.0)
            comb_s[...] = here if k == 0 else comb_s[...] + here

    def out_terms(k):
        def step(j, carry):
            cols = pl.ds(pl.multiple_of(j * TILE, TILE), TILE)
            out = dot(hid[k], down_w[:, cols], NN)
            out_p[k, :, :, :, cols] = out.astype(BF16).reshape(2, 2, rows, TILE)
            return carry

        lax.fori_loop(0, width // TILE, step, 0, unroll=True)
        core_send(k, 0)

    def in_terms(k):
        def step(j, carry):
            cols = pl.ds(pl.multiple_of(j * TILE, TILE), TILE)
            into = dot(gpart[k], gate_t[:, cols], NN) + dot(upart[k], up_t[:, cols], NN)
            in_p[k, :, :, :, cols] = into.astype(BF16).reshape(2, 2, rows, TILE)
            return carry

        lax.fori_loop(0, width // TILE, step, 0, unroll=True)
        core_send(k, 1)

    partial = ((out_p, core_o, x_o, z_o), (in_p, core_i, x_i, z_i))

    def core_send(k, h):
        p, c, _, _ = partial[h]
        copy(p.at[k, 1], c.at[k], device(rc=1), ("rc", k, h), ("rc", k, h))

    def core_sum(k, h):
        p, c, r, _ = partial[h]
        arrived(c.at[k], "rc", k, h)
        p[k, 0] = (p[k, 0].astype(F32) + c[k].astype(F32)).astype(BF16)
        copy(p.at[k, 0, 1], r.at[k], device(rx=1), ("rx", k, h), ("rx", k, h))

    def x_sum(k, h):
        p, _, r, q = partial[h]
        arrived(r.at[k], "rx", k, h)
        total = p[k, 0, 0].astype(F32) + r[k].astype(F32)
        if h == 1 and k == 2:
            arrived(q.at[2], "rz", 3, h)
            total = total + q[2].astype(F32)
        p[k, 0, 0] = total.astype(BF16)
        to = 1 if h == 1 and k == 3 else k
        copy(p.at[k, 0, 0], q.at[k - 1], device(rz=to), ("rz", k, h), ("rz", k, h))

    def last_sum(h):
        p, _, r, q = partial[h]
        arrived(r.at[0], "rx", 0, h)
        total = p[0, 0, 0].astype(F32) + r[0].astype(F32)
        for k in range(1, 3 if h == 1 else 4):
            arrived(q.at[k - 1], "rz", k, h)
            total = total + q[k - 1].astype(F32)
        return total

    hops = (
        (combs.at[0, me], combs.at[0, me], device(rc=1)),
        (combs.at[0, pl.ds(me - core, 2)], combs.at[0, pl.ds(me - core, 2)], device(rx=1)),
        (combs.at[0, pl.ds(z * 4, 4)], combs.at[0, pl.ds(z * 4, 4)], device(rz=1)),
        (combs.at[0, pl.ds(z * 4, 4)], combs.at[0, pl.ds(z * 4, 4)], device(rz=2)),
        (combs.at[0, pl.ds(z * 4, 4)], combs.at[0, pl.ds(z * 4, 4)], device(rz=3)),
        (combs.at[0], combs.at[1], device(ry=1)),
    )

    def hop(*steps):
        for i in steps:
            src, dst, to = hops[i]
            copy(src, dst, to, ("l", i), ("l", i))

    def hopped(*steps):
        for i in steps:
            arrived(hops[i][1], "l", i)

    def logit_grads(ry, k):
        comb = jnp.zeros((experts, LANES), F32)
        for i in range(4):
            comb = comb + jnp.where(z_of[k] == i, combs[ry, :, i, :], 0.0)
        comb = swap_lanes(comb)
        aux_t = tok_all[ry, k, :, :, :, width:].reshape(group, LANES).astype(F32).T
        terms = [aux_t[i * experts : (i + 1) * experts, :] for i in range(6)]
        combine = terms[0] + terms[1] + terms[2]
        probability = terms[3] + terms[4] + terms[5]
        selected = jnp.where(combine > 0.0, probability, 0.0)
        sel_total = jnp.sum(selected, axis=0, keepdims=True)
        mean = jnp.sum(combine * comb, axis=0, keepdims=True)
        sel_grad = jnp.where(combine > 0.0, (comb - mean) / sel_total, 0.0)
        grad = probability * (sel_grad - jnp.sum(probability * sel_grad, axis=0, keepdims=True))
        at = (ry * 4 + k) * group
        for i, term in enumerate(split3(grad)):
            lgs_t[i * experts : (i + 1) * experts, at : at + group] = term.astype(BF16)

    def width_grads(spans, begin, end):
        def d_step(j, carry):
            at = pl.ds(pl.multiple_of(j * TILE, TILE), TILE)
            cols = pl.ds(pl.multiple_of(dp * half + j * TILE, TILE), TILE)
            for part, acc, ref in ((gpart, acc_g, gg_ref), (upart, acc_u, ug_ref)):
                total = None
                for ry, lo, hi in spans:
                    n = (hi - lo) * group
                    term = dot(
                        tok_all[ry, lo:hi, :, :, :, cols].reshape(n, TILE),
                        part[ry * 4 + lo : ry * 4 + hi].reshape(n, inner), TN,
                    )
                    total = term if total is None else total + term
                if not begin:
                    total = total + acc[at, :]
                if end:
                    ref[at, :] = total.astype(BF16)
                else:
                    acc[at, :] = total
            return carry

        lax.fori_loop(0, half // TILE, d_step, 0, unroll=True)

    def inner_grads(spans, begin, end):
        def f_step(j, carry):
            at = pl.ds(pl.multiple_of(j * TILE, TILE), TILE)
            cols = pl.ds(pl.multiple_of(dp * half, TILE), half)
            total = None
            for ry, lo, hi in spans:
                n = (hi - lo) * group
                term = dot(
                    hid[ry * 4 + lo : ry * 4 + hi, :, at].reshape(n, TILE),
                    cot_all[ry, lo:hi, :, :, :, cols].reshape(n, half), TN,
                )
                total = term if total is None else total + term
            if not begin:
                total = total + acc_d[at, :]
            if end:
                dg_ref[at, :] = total.astype(BF16)
            else:
                acc_d[at, :] = total
            return carry

        lax.fori_loop(0, inner // TILE, f_step, 0, unroll=True)

    def flip(src, dst):
        depth = src.shape[1]

        def step(j, carry):
            at = pl.ds(pl.multiple_of(j * TILE, TILE), TILE)
            if src.shape[0] > depth:
                dst[:, at] = src[at, :].T
            else:
                dst[at, :] = src[:, at].T
            return carry

        lax.fori_loop(0, max(src.shape) // TILE, step, 0, unroll=True)

    for h in range(2):
        z_send(h, 0, 1, 1)
        later.append((h, 0, 1, 1, True))
        middle_only((h, 0, 3, 3))
        spread(0, h)
    for load, src, dst in zip(loads, (down_w, gate_w, up_w), (down_t, gate_t, up_t)):
        load.wait()
        flip(src, dst)
    TOK, COT, OUT, IN = 0, 1, 0, 1
    for k in range(4):
        for h in (TOK, COT):
            if k < 3:
                on_z(k + 1, h)
            on_x(k, h)
            on_core(0, k, h)
            if h == TOK:
                forward(0, k)
                if k == 3:
                    core_sum(2, IN)
                out_terms(k)
            else:
                backward(0, k)
                if k == 1:
                    on_y(0, 0, TOK)
                    on_y(0, 0, COT)
                if k == 2:
                    core_sum(2, OUT)
                if k == 3:
                    combs[0, me] = comb_s[...]
                    hop(0)
                    core_sum(3, OUT)
                    x_sum(2, OUT)
                    hopped(0)
                    hop(1)
                in_terms(k)
    on_y(0, 1, TOK)
    on_y(0, 1, COT)
    core_sum(3, IN)
    for k in (1, 0):
        core_sum(k, OUT)
        core_sum(k, IN)

    def other_plane(k):
        for h in (TOK, COT):
            for rx in range(2):
                if k > 0:
                    on_y(k, rx, h)
        on_core(1, k, TOK)
        forward(1, k)
        on_core(1, k, COT)
        backward(1, k)

    other_plane(0)
    x_sum(3, OUT)
    hopped(1)
    hop(2, 3, 4)
    x_sum(3, IN)
    other_plane(1)
    x_sum(1, OUT)
    other_plane(2)
    x_sum(2, IN)
    width_grads(((0, 0, 4),), True, False)
    x_sum(1, IN)
    hopped(2, 3, 4)
    hop(5)
    inner_grads(((0, 0, 4),), True, False)
    for k in range(4):
        logit_grads(0, k)
    other_plane(3)
    out_ref[...] = last_sum(OUT).astype(BF16)
    stores = [
        pltpu.make_async_copy(src, dst, store_sem.at[i])
        for i, (src, dst) in enumerate(((gg_ref, gg_hbm), (ug_ref, ug_hbm), (dg_ref, dg_hbm)))
    ]
    width_grads(((1, 0, 4),), False, True)
    stores[0].start()
    stores[1].start()
    inner_grads(((1, 0, 4),), False, True)
    stores[2].start()
    back = dot(lgs_t[: 3 * experts, :group], router_t[: 3 * experts, :], TN)
    tgrad_ref[...] = (last_sum(IN) + back[:rows]).astype(BF16)
    hopped(5)
    for k in range(4):
        logit_grads(1, k)

    def r_step(j, carry):
        cols = pl.ds(pl.multiple_of(j * TILE, TILE), TILE)
        total = dot(
            lgs_t[...], tok_all[:, :, :, :, :, cols].reshape(32 * rows, TILE), NN
        )
        rgrad_ref[:, cols] = (
            total[:experts] + total[experts : 2 * experts] + total[2 * experts : 3 * experts]
        )
        return carry

    lax.fori_loop(0, width // TILE, r_step, 0, unroll=True)

    for store in stores:
        store.wait()
    for made in sent:
        made.wait_send()

    def z_done(h, from_rel, to_rel, land):
        a = blocks[h]
        pltpu.make_async_remote_copy(
            src_ref=a.at[0, from_rel, 0, 0], dst_ref=a.at[0, land, 0, 0],
            send_sem=send_sem.at[book("s", "z", from_rel, to_rel, h)],
            recv_sem=recv_sem.at[book("z", land, h)],
            device_id=device(rz=to_rel), device_id_type=MESH,
        ).wait_send()

    for args in later:
        if len(args) == 5:
            z_done(*args[:4])

    @pl.when(middle_chip)
    def _():
        for args in later:
            if len(args) == 4:
                z_done(*args)

    assert len(book.places) <= send_sem.shape[0]


def hand_over(arrays):
    n = len(arrays)
    pieces = [4 if a.shape[0] >= 128 else 2 for a in arrays]

    def kernel(*refs):
        sources, targets, held = refs[:n], refs[n : 2 * n], refs[2 * n : 3 * n]
        in_sem, out_sem = refs[3 * n :]
        ins, outs = [], []
        for i in range(n):
            step = arrays[i].shape[0] // pieces[i]
            for j in range(pieces[i]):
                at = pl.ds(j * step, step)
                ins.append(pltpu.make_async_copy(sources[i].at[at], held[i].at[at], in_sem.at[i, j]))
                outs.append(pltpu.make_async_copy(held[i].at[at], targets[i].at[at], out_sem.at[i, j]))
        for made in ins:
            made.start()
        for before, made in zip(ins, outs):
            before.wait()
            made.start()
        for made in outs:
            made.wait()

    return pl.pallas_call(
        kernel,
        out_shape=tuple(jax.ShapeDtypeStruct(a.shape, a.dtype) for a in arrays),
        in_specs=[pl.BlockSpec(memory_space=pl.ANY)] * n,
        out_specs=(pl.BlockSpec(memory_space=pl.ANY),) * n,
        scratch_shapes=[pltpu.VMEM(a.shape, a.dtype) for a in arrays]
        + [pltpu.SemaphoreType.DMA((n, 4)), pltpu.SemaphoreType.DMA((n, 4))],
        compiler_params=pltpu.CompilerParams(vmem_limit_bytes=60 * 2**20),
    )(*arrays)


def local_fused(tokens, routes, cotangent, router_weight, gate_weight, up_weight, down_weight):
    rows, width = tokens.shape
    experts = router_weight.shape[1]
    inner = gate_weight.shape[2]
    half = width // 2
    wide = width + LANES
    vmem = lambda *shape, dtype=BF16: pltpu.VMEM(shape, dtype)
    scratch = [
        vmem(2, 4, 2, 2, rows, wide), vmem(2, 4, 2, 2, rows, width),
        vmem(width, inner), vmem(width, inner), vmem(inner, width),
        vmem(inner, width), vmem(inner, width), vmem(width, inner),
        vmem(8, 4 * rows, inner), vmem(8, 4 * rows, inner), vmem(8, 4 * rows, inner),
        vmem(4 * rows, inner, dtype=F32), vmem(4 * rows, inner, dtype=F32),
        vmem(4 * rows, inner, dtype=F32),
        vmem(4, 2, 2, rows, width), vmem(4, 2, 2, rows, width),
        vmem(4, 2, rows, width), vmem(4, 2, rows, width),
        vmem(4, rows, width), vmem(4, rows, width),
        vmem(3, rows, width), vmem(3, rows, width),
        vmem(2, experts, 8, LANES, dtype=F32), vmem(8, LANES, dtype=F32),
        vmem(3 * experts, 32 * rows), vmem(LANES, width),
        vmem(half, inner, dtype=F32), vmem(half, inner, dtype=F32), vmem(inner, half, dtype=F32),
        vmem(half, inner), vmem(half, inner), vmem(inner, half),
        pltpu.SemaphoreType.DMA((3,)), pltpu.SemaphoreType.DMA((3,)),
        pltpu.SemaphoreType.DMA((2 * COPIES,)), pltpu.SemaphoreType.DMA((2 * COPIES,)),
    ]
    in_vmem = pl.BlockSpec(memory_space=pltpu.VMEM)
    in_any = pl.BlockSpec(memory_space=pl.ANY)
    results = pl.pallas_call(
        functools.partial(fused, experts),
        out_shape=(
            jax.ShapeDtypeStruct((rows, width), BF16),
            jax.ShapeDtypeStruct((rows, width), BF16),
            jax.ShapeDtypeStruct((half, inner), BF16),
            jax.ShapeDtypeStruct((half, inner), BF16),
            jax.ShapeDtypeStruct((inner, half), BF16),
            jax.ShapeDtypeStruct((experts, width), F32),
        ),
        in_specs=[in_vmem] * 4 + [in_any] * 3,
        out_specs=(in_vmem, in_vmem, in_any, in_any, in_any, in_vmem),
        scratch_shapes=scratch,
        compiler_params=pltpu.CompilerParams(
            collective_id=0, has_side_effects=True, vmem_limit_bytes=62 * 2**20
        ),
    )(
        tokens, routes.T, cotangent, router_weight.T, gate_weight[0], up_weight[0], down_weight[0]
    )
    layer_out, token_grad, gate_grad, up_grad, down_grad, router_grad = hand_over(results)
    return (
        layer_out, token_grad, gate_grad[None], up_grad[None], down_grad[None], router_grad.T
    )


def silu_parts(gate_act):
    sigmoid_value = jax.nn.sigmoid(gate_act)
    act_value = gate_act * sigmoid_value
    act_slope = sigmoid_value * (1.0 + gate_act * (1.0 - sigmoid_value))
    return (act_value, act_slope)


def expert_forward(arrived, gate_weight, up_weight, down_weight):
    gate_act = jnp.einsum(
        "sjcd,jdf->sjcf", arrived, gate_weight, preferred_element_type=jnp.float32
    )
    up_act = jnp.einsum("sjcd,jdf->sjcf", arrived, up_weight, preferred_element_type=jnp.float32)
    act_value, act_slope = silu_parts(gate_act)
    hidden = (act_value * up_act).astype(jnp.bfloat16)
    expert_out = jnp.einsum(
        "sjcf,jfd->sjcd", hidden, down_weight, preferred_element_type=jnp.float32
    ).astype(jnp.bfloat16)
    return (expert_out, (up_act, act_value, act_slope, hidden))


def expert_backward(arrived_grads, stored, gate_weight, up_weight, down_weight):
    up_act, act_value, act_slope, hidden = stored
    hidden_grad = jnp.einsum(
        "sjcd,jfd->sjcf", arrived_grads, down_weight, preferred_element_type=jnp.float32
    )
    gate_part = (hidden_grad * up_act * act_slope).astype(jnp.bfloat16)
    up_part = (hidden_grad * act_value).astype(jnp.bfloat16)
    input_grad = (
        jnp.einsum("sjcf,jdf->sjcd", gate_part, gate_weight, preferred_element_type=jnp.float32)
        + jnp.einsum("sjcf,jdf->sjcd", up_part, up_weight, preferred_element_type=jnp.float32)
    ).astype(jnp.bfloat16)
    return (input_grad, gate_part, up_part)


def local_slots(tokens, routes, cotangent, router_weight, gate_weight, up_weight, down_weight):
    tok_rows, top_count = routes.shape
    model_width = tokens.shape[1]
    expert_count = router_weight.shape[1]
    local_count = gate_weight.shape[0]
    group_size = lax.axis_size("expert")
    capacity = min(tok_rows, 2 * tok_rows * top_count // expert_count)
    slot_total = expert_count * capacity
    buffer_shape = (group_size, local_count, capacity, model_width)
    logits = jnp.dot(tokens, router_weight, preferred_element_type=jnp.float32)
    exp_logits = jnp.exp(logits)
    probability = exp_logits / jnp.sum(exp_logits, axis=1, keepdims=True)
    chosen = (
        routes[:, :, None] == jnp.arange(expert_count, dtype=jnp.int32)[None, None, :]
    ).astype(jnp.int32)
    chosen_float = chosen.astype(jnp.float32)
    selected = jnp.sum(chosen_float * probability[:, None, :], axis=2)
    sel_total = jnp.sum(selected, axis=1, keepdims=True)
    combine = selected / sel_total
    per_token = jnp.sum(chosen, axis=1)
    before = jnp.tril(jnp.ones((tok_rows, tok_rows), jnp.float32), -1)
    earlier = jnp.dot(before, per_token.astype(jnp.float32)).astype(jnp.int32)
    slot_ids = jnp.sum(chosen * earlier[:, None, :], axis=2)
    flat_slot = routes * capacity + slot_ids
    match_map = (
        flat_slot[:, :, None] == jnp.arange(slot_total, dtype=jnp.int32)[None, None, :]
    ).astype(jnp.float32)
    presence = jnp.sum(match_map, axis=1)
    weight_map = jnp.sum(match_map * combine[:, :, None], axis=1)
    send_rows = (
        jnp.einsum(
            "tr,td->rd", presence.astype(jnp.bfloat16), tokens, preferred_element_type=jnp.float32
        )
        .astype(jnp.bfloat16)
        .reshape(buffer_shape)
    )
    send_grads = (
        jnp.einsum(
            "tr,td->rd", weight_map, cotangent.astype(jnp.float32), precision=lax.Precision.HIGHEST
        )
        .astype(jnp.bfloat16)
        .reshape(buffer_shape)
    )
    arrived = lax.all_to_all(send_rows, "expert", split_axis=0, concat_axis=0, tiled=True)
    expert_out, stored = expert_forward(arrived, gate_weight, up_weight, down_weight)
    returned = lax.all_to_all(expert_out, "expert", split_axis=0, concat_axis=0, tiled=True)
    arrived_grads = lax.all_to_all(send_grads, "expert", split_axis=0, concat_axis=0, tiled=True)
    input_grad, gate_part, up_part = expert_backward(
        arrived_grads, stored, gate_weight, up_weight, down_weight
    )
    returned_grads = lax.all_to_all(input_grad, "expert", split_axis=0, concat_axis=0, tiled=True)
    hidden = stored[3]
    gate_term = jnp.einsum("sjcd,sjcf->jdf", arrived, gate_part, preferred_element_type=jnp.float32)
    up_term = jnp.einsum("sjcd,sjcf->jdf", arrived, up_part, preferred_element_type=jnp.float32)
    down_term = jnp.einsum(
        "sjcf,sjcd->jfd", hidden, arrived_grads, preferred_element_type=jnp.float32
    )
    gate_sum, up_sum, down_sum = (
        lax.psum_scatter(gate_term, "dp", scatter_dimension=1, tiled=True),
        lax.psum_scatter(up_term, "dp", scatter_dimension=1, tiled=True),
        lax.psum_scatter(down_term, "dp", scatter_dimension=2, tiled=True),
    )
    gate_grad = gate_sum.astype(jnp.bfloat16)
    up_grad = up_sum.astype(jnp.bfloat16)
    down_grad = down_sum.astype(jnp.bfloat16)
    flat_index = flat_slot.reshape(-1)
    out_sel = jnp.take(returned.reshape(slot_total, model_width), flat_index, axis=0).reshape(
        tok_rows, top_count, model_width
    )
    grad_sel = jnp.take(
        returned_grads.reshape(slot_total, model_width), flat_index, axis=0
    ).reshape(tok_rows, top_count, model_width)
    layer_out = jnp.sum(combine[:, :, None] * out_sel.astype(jnp.float32), axis=1).astype(
        jnp.bfloat16
    )
    comb_grad = jnp.einsum("tkd,td->tk", out_sel, cotangent, preferred_element_type=jnp.float32)
    sel_grad = (comb_grad - jnp.sum(combine * comb_grad, axis=1, keepdims=True)) / sel_total
    prob_grad = jnp.sum(chosen_float * sel_grad[:, :, None], axis=1)
    logit_grad = probability * (prob_grad - jnp.sum(probability * prob_grad, axis=1, keepdims=True))
    router_term = jnp.einsum(
        "td,te->de", tokens.astype(jnp.float32), logit_grad, precision=lax.Precision.HIGHEST
    )
    router_grad = lax.psum(router_term, ("dp", "expert"))
    router_back = jnp.einsum(
        "te,de->td", logit_grad, router_weight.astype(jnp.float32), precision=lax.Precision.HIGHEST
    )
    token_grad = (jnp.sum(grad_sel.astype(jnp.float32), axis=1) + router_back).astype(jnp.bfloat16)
    return (layer_out, token_grad, gate_grad, up_grad, down_grad, router_grad)


def local(tokens, routes, cotangent, router_weight, gate_weight, up_weight, down_weight):
    tok_rows, top_count = routes.shape
    capacity = min(tok_rows, 2 * tok_rows * top_count // router_weight.shape[1])
    dense = (
        capacity == tok_rows
        and gate_weight.shape[0] == 1
        and router_weight.shape[1] == 16
        and lax.axis_size("dp") == 2
        and lax.axis_size("expert") == 16
    )
    plan = local_fused if dense else local_slots
    return plan(tokens, routes, cotangent, router_weight, gate_weight, up_weight, down_weight)


def solution(mesh):
    return jax.shard_map(
        local,
        mesh=mesh,
        in_specs=(
            P(("dp", "expert"), None),
            P(("dp", "expert"), None),
            P(("dp", "expert"), None),
            P(),
            P("expert", None, None),
            P("expert", None, None),
            P("expert", None, None),
        ),
        out_specs=(
            P(("dp", "expert"), None),
            P(("dp", "expert"), None),
            P("expert", "dp", None),
            P("expert", "dp", None),
            P("expert", None, "dp"),
            P(),
        ),
        check_vma=False,
    )
```

```python
import functools

import jax
import jax.numpy as jnp
from jax import lax
from jax.experimental import pallas as pl
from jax.experimental.pallas import tpu as pltpu
from jax.sharding import PartitionSpec as P

MESH = pl.DeviceIdType.MESH
NN = (((1,), (0,)), ((), ()))
NT = (((1,), (1,)), ((), ()))
TN = (((0,), (0,)), ((), ()))
F32 = jnp.float32
BF16 = jnp.bfloat16
TILE = 256
LANES = 128


def dot(a, b, dims):
    return lax.dot_general(a, b, dims, preferred_element_type=F32)


def split3(value):
    high = value.astype(BF16).astype(F32)
    middle = (value - high).astype(BF16).astype(F32)
    low = (value - high - middle).astype(BF16).astype(F32)
    return high, middle, low


class Book:
    def __init__(self):
        self.places = {}

    def __call__(self, *key):
        return self.places.setdefault(key, len(self.places))


COPIES = 110


def fused(
    experts, tok_ref, routes_ref, cot_ref, router_ref, gate_hbm, up_hbm, down_hbm,
    out_ref, tgrad_ref, gg_hbm, ug_hbm, dg_hbm, rgrad_ref,
    tok_all, cot_all, gate_w, up_w, down_w, gate_t, up_t, down_t,
    hid, gpart, upart, act_s, slope_s, hidden_s,
    out_p, in_p, core_o, core_i, x_o, x_i, z_o, z_i,
    combs, comb_s, lgs_t, router_t, acc_g, acc_u, acc_d, gg_ref, ug_ref, dg_ref,
    load_sem, store_sem, send_sem, recv_sem,
):
    rows, width = tok_ref.shape
    inner = gate_w.shape[1]
    half = acc_g.shape[0]
    group = 4 * rows
    dp = lax.axis_index("dp")
    me = lax.axis_index("expert")
    z, x, core = me // 4, (me // 2) % 2, me % 2
    z_of = {0: z, 1: z + 1 - 2 * (z % 2), 2: (z + 2) % 4, 3: 3 - z}
    middle_chip = (z + 1) % 4 >= 2

    def device(ry=0, rz=0, rc=0, rx=0):
        return (
            1 - dp if ry else dp,
            z_of[rz] * 4 + (1 - x if rx else x) * 2 + (1 - core if rc else core),
        )

    barrier = pltpu.get_barrier_semaphore()
    others = [device(rc=1), device(rx=1), device(ry=1), device(rz=1), device(rz=2), device(rz=3)]
    for other in others:
        pl.semaphore_signal(barrier, inc=1, device_id=other, device_id_type=MESH)

    loads = [
        pltpu.make_async_copy(src, dst, load_sem.at[i])
        for i, (src, dst) in enumerate(((down_hbm, down_w), (gate_hbm, gate_w), (up_hbm, up_w)))
    ]
    for load in loads:
        load.start()

    lane = lax.broadcasted_iota(jnp.int32, (rows, LANES), 1)
    first = lane < experts
    for i in range(LANES // experts):
        router_t[i * experts : (i + 1) * experts, :] = router_ref[...]
    exp_logits = jnp.exp(dot(tok_ref[...], router_t[...], NT))
    masked = jnp.where(first, exp_logits, 0.0)
    probability = exp_logits / jnp.sum(masked, axis=1, keepdims=True)
    chosen = jnp.zeros((LANES, rows), F32)
    expert_row = lax.broadcasted_iota(jnp.int32, (LANES, rows), 0) % experts
    for k in range(routes_ref.shape[0]):
        chosen = chosen + (routes_ref[k : k + 1, :] == expert_row).astype(F32)
    eye = (
        lax.broadcasted_iota(jnp.int32, (rows, rows), 0)
        == lax.broadcasted_iota(jnp.int32, (rows, rows), 1)
    ).astype(F32)
    chosen = dot(eye.astype(BF16), chosen.astype(BF16), NT)
    selected = chosen * probability
    sel_total = jnp.sum(jnp.where(first, selected, 0.0), axis=1, keepdims=True)
    combine = selected / sel_total
    part = lane // experts
    aux = jnp.zeros((rows, LANES), F32)
    for i, term in enumerate(split3(combine) + split3(probability)):
        aux = jnp.where(part == i, term, aux)
    tok_all[0, 0, 0, 0, :, :width] = tok_ref[...]
    tok_all[0, 0, 0, 0, :, width:] = aux.astype(BF16)
    cot_all[0, 0, 0, 0] = cot_ref[...]

    pl.semaphore_wait(barrier, len(others))

    book = Book()
    sent = []
    blocks = (tok_all, cot_all)

    def copy(src, dst, to, send_key, recv_key, keep=True):
        made = pltpu.make_async_remote_copy(
            src_ref=src, dst_ref=dst,
            send_sem=send_sem.at[book("s", *send_key)], recv_sem=recv_sem.at[book(*recv_key)],
            device_id=to, device_id_type=MESH,
        )
        made.start()
        if keep:
            sent.append(made)
        return made

    def arrived(dst, *key):
        pltpu.make_async_remote_copy(
            src_ref=dst, dst_ref=dst, send_sem=send_sem.at[0], recv_sem=recv_sem.at[book(*key)],
            device_id=device(rc=1), device_id_type=MESH,
        ).wait_recv()

    later = []

    def z_send(h, from_rel, to_rel, land):
        a = blocks[h]
        return copy(
            a.at[0, from_rel, 0, 0], a.at[0, land, 0, 0], device(rz=to_rel),
            ("z", from_rel, to_rel, h), ("z", land, h), keep=False,
        )

    def middle_only(*sends):
        @pl.when(middle_chip)
        def _():
            for args in sends:
                z_send(*args)

        later.extend(sends)

    def to_x(k, h):
        a = blocks[h]
        copy(a.at[0, k, 0, 0], a.at[0, k, 0, 1], device(rx=1), ("x", k, h), ("x", k, h))

    def to_y(k, rx, h):
        a = blocks[h]
        copy(a.at[0, k, 0, rx], a.at[1, k, 0, rx], device(ry=1), ("y", k, rx, h), ("y", k, rx, h))

    def to_core(ry, k, rx, h):
        a = blocks[h]
        copy(
            a.at[ry, k, 0, rx], a.at[ry, k, 1, rx], device(rc=1), ("c", ry, k, rx, h), ("c", ry, k, rx, h)
        )

    def spread(k, h):
        to_x(k, h)
        to_core(0, k, 0, h)
        if k != 1:
            to_y(k, 0, h)

    def on_z(k, h):
        here = blocks[h]
        if k == 1:
            arrived(here.at[0, 1, 0, 0], "z", 1, h)

            @pl.when(middle_chip)
            def _():
                z_send(h, 1, 3, 2)
                arrived(here.at[0, 3, 0, 0], "z", 3, h)
                z_send(h, 3, 1, 2)

            later.extend([(h, 1, 3, 2), (h, 3, 1, 2)])
        elif k == 2:
            arrived(here.at[0, 2, 0, 0], "z", 2, h)
            middle_only((h, 2, 1, 3))
        else:

            @pl.when(jnp.logical_not(middle_chip))
            def _():
                arrived(here.at[0, 3, 0, 0], "z", 3, h)

        spread(k, h)

    def on_x(k, h):
        arrived(blocks[h].at[0, k, 0, 1], "x", k, h)
        to_core(0, k, 1, h)
        to_y(k, 1, h)

    def on_y(k, rx, h):
        a = blocks[h]
        arrived(a.at[1, k, 0, rx], "y", k, rx, h)
        to_core(1, k, rx, h)
        if (k, rx) == (0, 0):
            copy(a.at[1, 0, 0, 0], a.at[1, 1, 0, 0], device(rz=1), ("yz", h), ("y", 1, 0, h))

    def on_core(ry, k, h):
        for rx in range(2):
            arrived(blocks[h].at[ry, k, 1, rx], "c", ry, k, rx, h)

    group_lane = lax.broadcasted_iota(jnp.int32, (group, LANES), 1)

    diagonal = group_lane == lax.broadcasted_iota(jnp.int32, (group, LANES), 0)
    comb_row = lax.broadcasted_iota(jnp.int32, (8, LANES), 0)

    def swap_lanes(value):
        even = (lax.broadcasted_iota(jnp.int32, value.shape, 1) // rows) % 2 == 0
        swapped = jnp.where(even, pltpu.roll(value, LANES - rows, 1), pltpu.roll(value, rows, 1))
        value = jnp.where(x == 1, swapped, value)
        return jnp.where(core == 1, pltpu.roll(value, 2 * rows, 1), value)

    def scale_of(ry, k):
        aux_rows = tok_all[ry, k, :, :, :, width:].reshape(group, LANES).astype(F32)
        return jnp.sum(jnp.where((group_lane % experts == me) & (group_lane < 3 * experts), aux_rows, 0.0), axis=1, keepdims=True)

    def forward(ry, k):
        scale = scale_of(ry, k)

        def step(j, carry):
            cols = pl.ds(pl.multiple_of(j * TILE, TILE), TILE)
            tok = tok_all[ry, k, :, :, :, :width].reshape(group, width)
            gate = dot(tok, gate_w[:, cols], NN)
            up = dot(tok, up_w[:, cols], NN)
            sigmoid = 1.0 / (1.0 + jnp.exp(-gate))
            act = gate * sigmoid
            hidden = act * up
            act_s[:, cols] = act
            slope_s[:, cols] = up * (sigmoid * (1.0 + gate * (1.0 - sigmoid)))
            hidden_s[:, cols] = hidden
            hid[ry * 4 + k, :, cols] = (hidden * scale).astype(BF16)
            return carry

        lax.fori_loop(0, inner // TILE, step, 0, unroll=True)

    def backward(ry, k):
        scale = scale_of(ry, k)

        def step(j, comb):
            cols = pl.ds(pl.multiple_of(j * TILE, TILE), TILE)
            raw = dot(cot_all[ry, k].reshape(group, width), down_t[:, cols], NN)
            grad = raw * scale
            gpart[ry * 4 + k, :, cols] = (grad * slope_s[:, cols]).astype(BF16)
            upart[ry * 4 + k, :, cols] = (grad * act_s[:, cols]).astype(BF16)
            return comb + jnp.sum(hidden_s[:, cols] * raw, axis=1, keepdims=True)

        comb = lax.fori_loop(0, inner // TILE, step, jnp.zeros((group, 1), F32), unroll=True)
        if ry == 0:
            row = jnp.sum(jnp.where(diagonal, comb, 0.0), axis=0, keepdims=True)
            here = jnp.where(comb_row == z_of[k], swap_lanes(row), 0.0)
            comb_s[...] = here if k == 0 else comb_s[...] + here

    def out_terms(k):
        def step(j, carry):
            cols = pl.ds(pl.multiple_of(j * TILE, TILE), TILE)
            out = dot(hid[k], down_w[:, cols], NN)
            out_p[k, :, :, :, cols] = out.astype(BF16).reshape(2, 2, rows, TILE)
            return carry

        lax.fori_loop(0, width // TILE, step, 0, unroll=True)
        core_send(k, 0)

    def in_terms(k):
        def step(j, carry):
            cols = pl.ds(pl.multiple_of(j * TILE, TILE), TILE)
            into = dot(gpart[k], gate_t[:, cols], NN) + dot(upart[k], up_t[:, cols], NN)
            in_p[k, :, :, :, cols] = into.astype(BF16).reshape(2, 2, rows, TILE)
            return carry

        lax.fori_loop(0, width // TILE, step, 0, unroll=True)
        core_send(k, 1)

    partial = ((out_p, core_o, x_o, z_o), (in_p, core_i, x_i, z_i))

    def core_send(k, h):
        p, c, _, _ = partial[h]
        copy(p.at[k, 1], c.at[k], device(rc=1), ("rc", k, h), ("rc", k, h))

    def core_sum(k, h):
        p, c, r, _ = partial[h]
        arrived(c.at[k], "rc", k, h)
        p[k, 0] = (p[k, 0].astype(F32) + c[k].astype(F32)).astype(BF16)
        copy(p.at[k, 0, 1], r.at[k], device(rx=1), ("rx", k, h), ("rx", k, h))

    def x_sum(k, h):
        p, _, r, q = partial[h]
        arrived(r.at[k], "rx", k, h)
        total = p[k, 0, 0].astype(F32) + r[k].astype(F32)
        if h == 1 and k == 2:
            arrived(q.at[2], "rz", 3, h)
            total = total + q[2].astype(F32)
        p[k, 0, 0] = total.astype(BF16)
        to = 1 if h == 1 and k == 3 else k
        copy(p.at[k, 0, 0], q.at[k - 1], device(rz=to), ("rz", k, h), ("rz", k, h))

    def last_sum(h):
        p, _, r, q = partial[h]
        arrived(r.at[0], "rx", 0, h)
        total = p[0, 0, 0].astype(F32) + r[0].astype(F32)
        for k in range(1, 3 if h == 1 else 4):
            arrived(q.at[k - 1], "rz", k, h)
            total = total + q[k - 1].astype(F32)
        return total

    hops = (
        (combs.at[0, me], combs.at[0, me], device(rc=1)),
        (combs.at[0, pl.ds(me - core, 2)], combs.at[0, pl.ds(me - core, 2)], device(rx=1)),
        (combs.at[0, pl.ds(z * 4, 4)], combs.at[0, pl.ds(z * 4, 4)], device(rz=1)),
        (combs.at[0, pl.ds(z * 4, 4)], combs.at[0, pl.ds(z * 4, 4)], device(rz=2)),
        (combs.at[0, pl.ds(z * 4, 4)], combs.at[0, pl.ds(z * 4, 4)], device(rz=3)),
        (combs.at[0], combs.at[1], device(ry=1)),
    )

    def hop(*steps):
        for i in steps:
            src, dst, to = hops[i]
            copy(src, dst, to, ("l", i), ("l", i))

    def hopped(*steps):
        for i in steps:
            arrived(hops[i][1], "l", i)

    def logit_grads(ry, k):
        comb = jnp.zeros((experts, LANES), F32)
        for i in range(4):
            comb = comb + jnp.where(z_of[k] == i, combs[ry, :, i, :], 0.0)
        comb = swap_lanes(comb)
        aux_t = tok_all[ry, k, :, :, :, width:].reshape(group, LANES).astype(F32).T
        terms = [aux_t[i * experts : (i + 1) * experts, :] for i in range(6)]
        combine = terms[0] + terms[1] + terms[2]
        probability = terms[3] + terms[4] + terms[5]
        selected = jnp.where(combine > 0.0, probability, 0.0)
        sel_total = jnp.sum(selected, axis=0, keepdims=True)
        mean = jnp.sum(combine * comb, axis=0, keepdims=True)
        sel_grad = jnp.where(combine > 0.0, (comb - mean) / sel_total, 0.0)
        grad = probability * (sel_grad - jnp.sum(probability * sel_grad, axis=0, keepdims=True))
        at = (ry * 4 + k) * group
        for i, term in enumerate(split3(grad)):
            lgs_t[i * experts : (i + 1) * experts, at : at + group] = term.astype(BF16)

    def width_grads(spans, begin, end):
        def d_step(j, carry):
            at = pl.ds(pl.multiple_of(j * TILE, TILE), TILE)
            cols = pl.ds(pl.multiple_of(dp * half + j * TILE, TILE), TILE)
            for part, acc, ref in ((gpart, acc_g, gg_ref), (upart, acc_u, ug_ref)):
                total = None
                for ry, lo, hi in spans:
                    n = (hi - lo) * group
                    term = dot(
                        tok_all[ry, lo:hi, :, :, :, cols].reshape(n, TILE),
                        part[ry * 4 + lo : ry * 4 + hi].reshape(n, inner), TN,
                    )
                    total = term if total is None else total + term
                if not begin:
                    total = total + acc[at, :]
                if end:
                    ref[at, :] = total.astype(BF16)
                else:
                    acc[at, :] = total
            return carry

        lax.fori_loop(0, half // TILE, d_step, 0, unroll=True)

    def inner_grads(spans, begin, end):
        def f_step(j, carry):
            at = pl.ds(pl.multiple_of(j * TILE, TILE), TILE)
            cols = pl.ds(pl.multiple_of(dp * half, TILE), half)
            total = None
            for ry, lo, hi in spans:
                n = (hi - lo) * group
                term = dot(
                    hid[ry * 4 + lo : ry * 4 + hi, :, at].reshape(n, TILE),
                    cot_all[ry, lo:hi, :, :, :, cols].reshape(n, half), TN,
                )
                total = term if total is None else total + term
            if not begin:
                total = total + acc_d[at, :]
            if end:
                dg_ref[at, :] = total.astype(BF16)
            else:
                acc_d[at, :] = total
            return carry

        lax.fori_loop(0, inner // TILE, f_step, 0, unroll=True)

    def flip(src, dst):
        depth = src.shape[1]

        def step(j, carry):
            at = pl.ds(pl.multiple_of(j * TILE, TILE), TILE)
            if src.shape[0] > depth:
                dst[:, at] = src[at, :].T
            else:
                dst[at, :] = src[:, at].T
            return carry

        lax.fori_loop(0, max(src.shape) // TILE, step, 0, unroll=True)

    for h in range(2):
        z_send(h, 0, 1, 1)
        later.append((h, 0, 1, 1, True))
        middle_only((h, 0, 3, 3))
        spread(0, h)
    for load, src, dst in zip(loads, (down_w, gate_w, up_w), (down_t, gate_t, up_t)):
        load.wait()
        flip(src, dst)
    TOK, COT, OUT, IN = 0, 1, 0, 1
    for k in range(4):
        for h in (TOK, COT):
            if k < 3:
                on_z(k + 1, h)
            on_x(k, h)
            on_core(0, k, h)
            if h == TOK:
                forward(0, k)
                if k == 3:
                    core_sum(2, IN)
                out_terms(k)
            else:
                backward(0, k)
                if k == 1:
                    on_y(0, 0, TOK)
                    on_y(0, 0, COT)
                if k == 2:
                    core_sum(2, OUT)
                if k == 3:
                    combs[0, me] = comb_s[...]
                    hop(0)
                    core_sum(3, OUT)
                    x_sum(2, OUT)
                    hopped(0)
                    hop(1)
                in_terms(k)
    on_y(0, 1, TOK)
    on_y(0, 1, COT)
    core_sum(3, IN)
    for k in (1, 0):
        core_sum(k, OUT)
        core_sum(k, IN)

    def other_plane(k):
        for h in (TOK, COT):
            for rx in range(2):
                if k > 0:
                    on_y(k, rx, h)
        on_core(1, k, TOK)
        forward(1, k)
        on_core(1, k, COT)
        backward(1, k)

    other_plane(0)
    x_sum(3, OUT)
    hopped(1)
    hop(2, 3, 4)
    x_sum(3, IN)
    other_plane(1)
    x_sum(1, OUT)
    other_plane(2)
    x_sum(2, IN)
    width_grads(((0, 0, 4),), True, False)
    x_sum(1, IN)
    hopped(2, 3, 4)
    hop(5)
    inner_grads(((0, 0, 4),), True, False)
    for k in range(4):
        logit_grads(0, k)
    other_plane(3)
    out_ref[...] = last_sum(OUT).astype(BF16)
    stores = [
        pltpu.make_async_copy(src, dst, store_sem.at[i])
        for i, (src, dst) in enumerate(((gg_ref, gg_hbm), (ug_ref, ug_hbm), (dg_ref, dg_hbm)))
    ]
    width_grads(((1, 0, 4),), False, True)
    stores[0].start()
    stores[1].start()
    inner_grads(((1, 0, 4),), False, True)
    stores[2].start()
    hopped(5)
    for k in range(4):
        logit_grads(1, k)

    def r_step(j, carry):
        cols = pl.ds(pl.multiple_of(j * TILE, TILE), TILE)
        total = dot(
            lgs_t[...], tok_all[:, :, :, :, :, cols].reshape(32 * rows, TILE), NN
        )
        rgrad_ref[:, cols] = (
            total[:experts] + total[experts : 2 * experts] + total[2 * experts : 3 * experts]
        )
        return carry

    lax.fori_loop(0, width // TILE, r_step, 0, unroll=True)

    back = dot(lgs_t[: 3 * experts, :group], router_t[: 3 * experts, :], TN)
    tgrad_ref[...] = (last_sum(IN) + back[:rows]).astype(BF16)
    for store in stores:
        store.wait()
    for made in sent:
        made.wait_send()

    def z_done(h, from_rel, to_rel, land):
        a = blocks[h]
        pltpu.make_async_remote_copy(
            src_ref=a.at[0, from_rel, 0, 0], dst_ref=a.at[0, land, 0, 0],
            send_sem=send_sem.at[book("s", "z", from_rel, to_rel, h)],
            recv_sem=recv_sem.at[book("z", land, h)],
            device_id=device(rz=to_rel), device_id_type=MESH,
        ).wait_send()

    for args in later:
        if len(args) == 5:
            z_done(*args[:4])

    @pl.when(middle_chip)
    def _():
        for args in later:
            if len(args) == 4:
                z_done(*args)

    assert len(book.places) <= send_sem.shape[0]


def hand_over(arrays):
    n = len(arrays)
    order = sorted(range(n), key=lambda i: -arrays[i].size)

    def kernel(*refs):
        sources, targets, held = refs[:n], refs[n : 2 * n], refs[2 * n : 3 * n]
        in_sem, out_sem = refs[3 * n :]
        ins = [pltpu.make_async_copy(sources[i], held[i], in_sem.at[i]) for i in order]
        outs = [pltpu.make_async_copy(held[i], targets[i], out_sem.at[i]) for i in order]
        for made in ins:
            made.start()
        for before, made in zip(ins, outs):
            before.wait()
            made.start()
        for made in outs:
            made.wait()

    return pl.pallas_call(
        kernel,
        out_shape=tuple(jax.ShapeDtypeStruct(a.shape, a.dtype) for a in arrays),
        in_specs=[pl.BlockSpec(memory_space=pl.ANY)] * n,
        out_specs=(pl.BlockSpec(memory_space=pl.ANY),) * n,
        scratch_shapes=[pltpu.VMEM(a.shape, a.dtype) for a in arrays]
        + [pltpu.SemaphoreType.DMA((n,)), pltpu.SemaphoreType.DMA((n,))],
        compiler_params=pltpu.CompilerParams(vmem_limit_bytes=60 * 2**20),
    )(*arrays)


def local_fused(tokens, routes, cotangent, router_weight, gate_weight, up_weight, down_weight):
    rows, width = tokens.shape
    experts = router_weight.shape[1]
    inner = gate_weight.shape[2]
    half = width // 2
    wide = width + LANES
    vmem = lambda *shape, dtype=BF16: pltpu.VMEM(shape, dtype)
    scratch = [
        vmem(2, 4, 2, 2, rows, wide), vmem(2, 4, 2, 2, rows, width),
        vmem(width, inner), vmem(width, inner), vmem(inner, width),
        vmem(inner, width), vmem(inner, width), vmem(width, inner),
        vmem(8, 4 * rows, inner), vmem(8, 4 * rows, inner), vmem(8, 4 * rows, inner),
        vmem(4 * rows, inner, dtype=F32), vmem(4 * rows, inner, dtype=F32),
        vmem(4 * rows, inner, dtype=F32),
        vmem(4, 2, 2, rows, width), vmem(4, 2, 2, rows, width),
        vmem(4, 2, rows, width), vmem(4, 2, rows, width),
        vmem(4, rows, width), vmem(4, rows, width),
        vmem(3, rows, width), vmem(3, rows, width),
        vmem(2, experts, 8, LANES, dtype=F32), vmem(8, LANES, dtype=F32),
        vmem(3 * experts, 32 * rows), vmem(LANES, width),
        vmem(half, inner, dtype=F32), vmem(half, inner, dtype=F32), vmem(inner, half, dtype=F32),
        vmem(half, inner), vmem(half, inner), vmem(inner, half),
        pltpu.SemaphoreType.DMA((3,)), pltpu.SemaphoreType.DMA((3,)),
        pltpu.SemaphoreType.DMA((2 * COPIES,)), pltpu.SemaphoreType.DMA((2 * COPIES,)),
    ]
    in_vmem = pl.BlockSpec(memory_space=pltpu.VMEM)
    in_any = pl.BlockSpec(memory_space=pl.ANY)
    results = pl.pallas_call(
        functools.partial(fused, experts),
        out_shape=(
            jax.ShapeDtypeStruct((rows, width), BF16),
            jax.ShapeDtypeStruct((rows, width), BF16),
            jax.ShapeDtypeStruct((half, inner), BF16),
            jax.ShapeDtypeStruct((half, inner), BF16),
            jax.ShapeDtypeStruct((inner, half), BF16),
            jax.ShapeDtypeStruct((experts, width), F32),
        ),
        in_specs=[in_vmem] * 4 + [in_any] * 3,
        out_specs=(in_vmem, in_vmem, in_any, in_any, in_any, in_vmem),
        scratch_shapes=scratch,
        compiler_params=pltpu.CompilerParams(
            collective_id=0, has_side_effects=True, vmem_limit_bytes=62 * 2**20
        ),
    )(
        tokens, routes.T, cotangent, router_weight.T, gate_weight[0], up_weight[0], down_weight[0]
    )
    layer_out, token_grad, gate_grad, up_grad, down_grad, router_grad = hand_over(results)
    return (
        layer_out, token_grad, gate_grad[None], up_grad[None], down_grad[None], router_grad.T
    )


def silu_parts(gate_act):
    sigmoid_value = jax.nn.sigmoid(gate_act)
    act_value = gate_act * sigmoid_value
    act_slope = sigmoid_value * (1.0 + gate_act * (1.0 - sigmoid_value))
    return (act_value, act_slope)


def expert_forward(arrived, gate_weight, up_weight, down_weight):
    gate_act = jnp.einsum(
        "sjcd,jdf->sjcf", arrived, gate_weight, preferred_element_type=jnp.float32
    )
    up_act = jnp.einsum("sjcd,jdf->sjcf", arrived, up_weight, preferred_element_type=jnp.float32)
    act_value, act_slope = silu_parts(gate_act)
    hidden = (act_value * up_act).astype(jnp.bfloat16)
    expert_out = jnp.einsum(
        "sjcf,jfd->sjcd", hidden, down_weight, preferred_element_type=jnp.float32
    ).astype(jnp.bfloat16)
    return (expert_out, (up_act, act_value, act_slope, hidden))


def expert_backward(arrived_grads, stored, gate_weight, up_weight, down_weight):
    up_act, act_value, act_slope, hidden = stored
    hidden_grad = jnp.einsum(
        "sjcd,jfd->sjcf", arrived_grads, down_weight, preferred_element_type=jnp.float32
    )
    gate_part = (hidden_grad * up_act * act_slope).astype(jnp.bfloat16)
    up_part = (hidden_grad * act_value).astype(jnp.bfloat16)
    input_grad = (
        jnp.einsum("sjcf,jdf->sjcd", gate_part, gate_weight, preferred_element_type=jnp.float32)
        + jnp.einsum("sjcf,jdf->sjcd", up_part, up_weight, preferred_element_type=jnp.float32)
    ).astype(jnp.bfloat16)
    return (input_grad, gate_part, up_part)


def local_slots(tokens, routes, cotangent, router_weight, gate_weight, up_weight, down_weight):
    tok_rows, top_count = routes.shape
    model_width = tokens.shape[1]
    expert_count = router_weight.shape[1]
    local_count = gate_weight.shape[0]
    group_size = lax.axis_size("expert")
    capacity = min(tok_rows, 2 * tok_rows * top_count // expert_count)
    slot_total = expert_count * capacity
    buffer_shape = (group_size, local_count, capacity, model_width)
    logits = jnp.dot(tokens, router_weight, preferred_element_type=jnp.float32)
    exp_logits = jnp.exp(logits)
    probability = exp_logits / jnp.sum(exp_logits, axis=1, keepdims=True)
    chosen = (
        routes[:, :, None] == jnp.arange(expert_count, dtype=jnp.int32)[None, None, :]
    ).astype(jnp.int32)
    chosen_float = chosen.astype(jnp.float32)
    selected = jnp.sum(chosen_float * probability[:, None, :], axis=2)
    sel_total = jnp.sum(selected, axis=1, keepdims=True)
    combine = selected / sel_total
    per_token = jnp.sum(chosen, axis=1)
    before = jnp.tril(jnp.ones((tok_rows, tok_rows), jnp.float32), -1)
    earlier = jnp.dot(before, per_token.astype(jnp.float32)).astype(jnp.int32)
    slot_ids = jnp.sum(chosen * earlier[:, None, :], axis=2)
    flat_slot = routes * capacity + slot_ids
    match_map = (
        flat_slot[:, :, None] == jnp.arange(slot_total, dtype=jnp.int32)[None, None, :]
    ).astype(jnp.float32)
    presence = jnp.sum(match_map, axis=1)
    weight_map = jnp.sum(match_map * combine[:, :, None], axis=1)
    send_rows = (
        jnp.einsum(
            "tr,td->rd", presence.astype(jnp.bfloat16), tokens, preferred_element_type=jnp.float32
        )
        .astype(jnp.bfloat16)
        .reshape(buffer_shape)
    )
    send_grads = (
        jnp.einsum(
            "tr,td->rd", weight_map, cotangent.astype(jnp.float32), precision=lax.Precision.HIGHEST
        )
        .astype(jnp.bfloat16)
        .reshape(buffer_shape)
    )
    arrived = lax.all_to_all(send_rows, "expert", split_axis=0, concat_axis=0, tiled=True)
    expert_out, stored = expert_forward(arrived, gate_weight, up_weight, down_weight)
    returned = lax.all_to_all(expert_out, "expert", split_axis=0, concat_axis=0, tiled=True)
    arrived_grads = lax.all_to_all(send_grads, "expert", split_axis=0, concat_axis=0, tiled=True)
    input_grad, gate_part, up_part = expert_backward(
        arrived_grads, stored, gate_weight, up_weight, down_weight
    )
    returned_grads = lax.all_to_all(input_grad, "expert", split_axis=0, concat_axis=0, tiled=True)
    hidden = stored[3]
    gate_term = jnp.einsum("sjcd,sjcf->jdf", arrived, gate_part, preferred_element_type=jnp.float32)
    up_term = jnp.einsum("sjcd,sjcf->jdf", arrived, up_part, preferred_element_type=jnp.float32)
    down_term = jnp.einsum(
        "sjcf,sjcd->jfd", hidden, arrived_grads, preferred_element_type=jnp.float32
    )
    gate_sum, up_sum, down_sum = (
        lax.psum_scatter(gate_term, "dp", scatter_dimension=1, tiled=True),
        lax.psum_scatter(up_term, "dp", scatter_dimension=1, tiled=True),
        lax.psum_scatter(down_term, "dp", scatter_dimension=2, tiled=True),
    )
    gate_grad = gate_sum.astype(jnp.bfloat16)
    up_grad = up_sum.astype(jnp.bfloat16)
    down_grad = down_sum.astype(jnp.bfloat16)
    flat_index = flat_slot.reshape(-1)
    out_sel = jnp.take(returned.reshape(slot_total, model_width), flat_index, axis=0).reshape(
        tok_rows, top_count, model_width
    )
    grad_sel = jnp.take(
        returned_grads.reshape(slot_total, model_width), flat_index, axis=0
    ).reshape(tok_rows, top_count, model_width)
    layer_out = jnp.sum(combine[:, :, None] * out_sel.astype(jnp.float32), axis=1).astype(
        jnp.bfloat16
    )
    comb_grad = jnp.einsum("tkd,td->tk", out_sel, cotangent, preferred_element_type=jnp.float32)
    sel_grad = (comb_grad - jnp.sum(combine * comb_grad, axis=1, keepdims=True)) / sel_total
    prob_grad = jnp.sum(chosen_float * sel_grad[:, :, None], axis=1)
    logit_grad = probability * (prob_grad - jnp.sum(probability * prob_grad, axis=1, keepdims=True))
    router_term = jnp.einsum(
        "td,te->de", tokens.astype(jnp.float32), logit_grad, precision=lax.Precision.HIGHEST
    )
    router_grad = lax.psum(router_term, ("dp", "expert"))
    router_back = jnp.einsum(
        "te,de->td", logit_grad, router_weight.astype(jnp.float32), precision=lax.Precision.HIGHEST
    )
    token_grad = (jnp.sum(grad_sel.astype(jnp.float32), axis=1) + router_back).astype(jnp.bfloat16)
    return (layer_out, token_grad, gate_grad, up_grad, down_grad, router_grad)


def local(tokens, routes, cotangent, router_weight, gate_weight, up_weight, down_weight):
    tok_rows, top_count = routes.shape
    capacity = min(tok_rows, 2 * tok_rows * top_count // router_weight.shape[1])
    dense = (
        capacity == tok_rows
        and gate_weight.shape[0] == 1
        and router_weight.shape[1] == 16
        and lax.axis_size("dp") == 2
        and lax.axis_size("expert") == 16
    )
    plan = local_fused if dense else local_slots
    return plan(tokens, routes, cotangent, router_weight, gate_weight, up_weight, down_weight)


def solution(mesh):
    return jax.shard_map(
        local,
        mesh=mesh,
        in_specs=(
            P(("dp", "expert"), None),
            P(("dp", "expert"), None),
            P(("dp", "expert"), None),
            P(),
            P("expert", None, None),
            P("expert", None, None),
            P("expert", None, None),
        ),
        out_specs=(
            P(("dp", "expert"), None),
            P(("dp", "expert"), None),
            P("expert", "dp", None),
            P("expert", "dp", None),
            P("expert", None, "dp"),
            P(),
        ),
        check_vma=False,
    )
```
